256 devices in a mesh: dp: 8 (over y, x_lo), ctx: 32 (over z, x_hi, core).
Axes of the slice: x: 4 (x_hi: 2, x_lo: 2; x = x_hi * 2 + x_lo), y: 4, z: 8, core: 2. Of those that a mesh axis runs over, the one named last changes fastest.
Arguments:
- queries: bfloat16 [8, 4096, 768], P('dp', 'ctx'), may hold values from -12 to 12
- attn_keys: bfloat16 [8, 4096, 768], P('dp', 'ctx'), may hold values from -6 to 6
- attn_values: bfloat16 [8, 4096, 768], P('dp', 'ctx'), may hold values from -6 to 6
- residual: bfloat16 [8, 4096, 1536], P('dp', 'ctx'), may hold values from -10 to 10
- out_weight: bfloat16 [768, 1536], P('dp'), may hold values from -0.21875 to 0.21875
- conv_taps: float32 [31, 1536], replicated, may hold values from -1 to 1
- norm_gain: float32 [1536], replicated, may hold values from 0.5 to 2
- lengths: int32 [8], P('dp'), may hold values from 1024 to 4096, as said below
- cotangent: bfloat16 [8, 4096, 1536], P('dp', 'ctx'), may hold values from -7 to 7
Outputs:
- layer_out: bfloat16 [8, 4096, 1536], P('dp', 'ctx')
- grad_queries: bfloat16 [8, 4096, 768], P('dp', 'ctx')
- grad_keys: bfloat16 [8, 4096, 768], P('dp', 'ctx')
- grad_values: bfloat16 [8, 4096, 768], P('dp', 'ctx')
- grad_residual: bfloat16 [8, 4096, 1536], P('dp', 'ctx')
- grad_weight: float32 [768, 1536], P('ctx', 'dp')
- grad_taps: float32 [31, 1536], replicated
- grad_gain: float32 [1536], replicated
The draws below stay inside these ranges and needn't reach their ends.
Inputs may be any that keep to these rules, and one draw needn't show every extreme that they name: Frames from lengths[u] on are padding; in every draw some utterance is whole.
All inputs are finite; a program needn't handle non-finite values.
Results may differ from the reference program's by a relative error of at most 0.035.
Values may be sent and summed in bfloat16 or wider, within the bound.
No kernel may reach another device: no remote copies, remote signals or barrier semaphores. Data moves between devices by JAX's collectives and lax.ppermute only.
A program may use at most 128 MiB of HBM per device.

```python
import math
import jax
import jax.numpy as jnp
from jax import lax

D = 1536
HEADS = 12
HD = 64
KTAPS = 31
FR_DEV = 128
HW = 768
UTT = 8
LEN = 4096
N_CTX = 32


def draw_attn_keys(key, part):
    key = jax.random.fold_in(key, 1)
    return jnp.clip(jax.random.normal(key, (UTT, LEN, HW), jnp.float32), -4.0, 4.0).astype(jnp.bfloat16)


def draw_queries(key, part):
    key = jax.random.fold_in(key, 2)
    return (2.0 * jnp.clip(jax.random.normal(key, (UTT, LEN, HW), jnp.float32), -4.0, 4.0)).astype(jnp.bfloat16)


def draw_residual(key, part):
    key = jax.random.fold_in(key, 3)
    row_key, col_key, base_key = jax.random.split(key, 3)
    row_scale = jnp.exp(jax.random.uniform(row_key, (UTT, LEN, 1), jnp.float32, math.log(0.3), math.log(1.5)))
    col_scale = jnp.exp(jax.random.uniform(col_key, (1, 1, D), jnp.float32, math.log(0.3), math.log(1.5)))
    return (jnp.clip(jax.random.normal(base_key, (UTT, LEN, D), jnp.float32), -4.0, 4.0) * row_scale * col_scale).astype(jnp.bfloat16)


def draw_cotangent(key, part):
    key = jax.random.fold_in(key, 4)
    position_frac = (jnp.arange(UTT)[:, None] * LEN + jnp.arange(LEN)[None, :]).astype(jnp.float32) / (UTT * LEN)
    ramp_scale = 0.5 * jnp.exp(position_frac * math.log(3.0))
    return (jnp.clip(jax.random.normal(key, (UTT, LEN, D), jnp.float32), -4.0, 4.0) * ramp_scale[:, :, None]).astype(jnp.bfloat16)


def draw_lengths(key, part):
    key = jax.random.fold_in(key, 5)
    base_key, pick_key = jax.random.split(key)
    base_draw = jax.random.randint(base_key, (UTT,), LEN // 4, LEN + 1)
    chosen = jax.random.randint(pick_key, (), 0, UTT)
    return jnp.where(jnp.arange(UTT) == chosen, LEN, base_draw).astype(jnp.int32)


def levels(key, dims, pieces, least, top_value):
    level, own = 1.0, jax.random.fold_in(key, 6)
    for position, shards_of in pieces:
        heights = jnp.exp(jax.random.uniform(jax.random.fold_in(own, position), (shards_of,), jnp.float32, least / len(pieces), top_value / len(pieces)))
        level = level * jnp.repeat(heights, dims[position] // shards_of).reshape([-1 if axis == position else 1 for axis in range(len(dims))])
    return level


def gaussian(own_key, dims, deviation, reach, pieces=(), kind=jnp.bfloat16):
    values = jax.random.normal(own_key, dims, jnp.float32) * deviation
    if len(pieces) > 0:
        values = levels(own_key, dims, pieces, -0.22, 0.18) * values
    return jnp.clip(values, min=-reach, max=reach).astype(kind)


def setup_inputs(seed: int = 0) -> dict:
    key_list = jax.random.split(jax.random.key(seed), 10)
    return {
        "queries": draw_queries(jax.random.fold_in(key_list[9], 71), 0),
        "attn_keys": draw_attn_keys(jax.random.fold_in(key_list[9], 71), 0),
        "attn_values": gaussian(key_list[2], (UTT, LEN, HW), 1.0, 6.0, ((0, 8), (1, 32))),
        "residual": draw_residual(jax.random.fold_in(key_list[9], 71), 0),
        "out_weight": gaussian(key_list[4], (HW, D), HW ** -0.5, 0.21875, ((0, 8),)),
        "conv_taps": gaussian(key_list[5], (KTAPS, D), KTAPS ** -0.5, 1.0, (), jnp.float32),
        "norm_gain": jnp.clip(jnp.exp(jax.random.uniform(key_list[6], (D,), jnp.float32, math.log(0.5), math.log(2.0))), 0.5, 2.0),
        "lengths": draw_lengths(jax.random.fold_in(key_list[9], 71), 0),
        "cotangent": draw_cotangent(jax.random.fold_in(key_list[9], 71), 0),
    }


MASK_FILL = -1e+30
NORM_EPSILON = 1e-05

def norm_part(mid_float, norm_gain, frame_valid):
    row_mean = lax.optimization_barrier(jnp.mean(mid_float, axis=-1, keepdims=True))
    centred = mid_float - row_mean
    spread = lax.optimization_barrier(jnp.mean(centred * centred, axis=-1, keepdims=True))
    return centred * lax.rsqrt(spread + NORM_EPSILON) * norm_gain * frame_valid

def depthwise(padded, conv_taps, frames):
    summed = jnp.zeros((padded.shape[0], frames, padded.shape[2]), jnp.float32)
    for offset in range(KTAPS):
        summed = summed + conv_taps[offset] * padded[:, offset:offset + frames].astype(jnp.float32)
    return summed

def tap_grads(padded, grad_conv, frames):
    rows_out = []
    for offset in range(KTAPS):
        window = padded[:, offset:offset + frames].astype(jnp.float32)
        rows_out.append(lax.optimization_barrier(jnp.sum(grad_conv.astype(jnp.float32) * window, axis=(0, 1))))
    return jnp.stack(rows_out)

def block_scores(query_block, key_all, key_valid):
    inv_root = 1.0 / math.sqrt(HD)
    query_heads = query_block.reshape(FR_DEV, HEADS, HD).astype(jnp.float32)
    key_heads = key_all.reshape(LEN, HEADS, HD).astype(jnp.float32)
    scores = jnp.einsum('qhd,khd->hqk', query_heads, key_heads) * inv_root
    return (jnp.where(key_valid[None, None, :], scores, MASK_FILL), query_heads, key_heads)

def forward_block(query_block, key_all, value_all, key_valid):
    scores, query_heads, key_heads = block_scores(query_block, key_all, key_valid)
    value_heads = value_all.reshape(LEN, HEADS, HD).astype(jnp.float32)
    row_max = lax.optimization_barrier(jnp.max(scores, axis=2, keepdims=True))
    shifted = jnp.exp(scores - row_max)
    row_sum = lax.optimization_barrier(jnp.sum(shifted, axis=2, keepdims=True))
    weights_bf = (shifted / row_sum).astype(jnp.bfloat16)
    attended = jnp.einsum('hqk,khd->qhd', weights_bf.astype(jnp.float32), value_heads)
    log_total = (row_max + jnp.log(row_sum))[:, :, 0]
    return (attended.reshape(FR_DEV, HW).astype(jnp.bfloat16), log_total.T)

def backward_block(query_block, datt_block, log_block, delta_block, key_all, value_all, key_valid):
    inv_root = 1.0 / math.sqrt(HD)
    scores, query_heads, key_heads = block_scores(query_block, key_all, key_valid)
    value_heads = value_all.reshape(LEN, HEADS, HD).astype(jnp.float32)
    datt_heads = datt_block.reshape(FR_DEV, HEADS, HD).astype(jnp.float32)
    prob = jnp.exp(scores - log_block.T[:, :, None])
    grad_prob = jnp.einsum('qhd,khd->hqk', datt_heads, value_heads)
    grad_score = (prob * (grad_prob - delta_block.T[:, :, None])).astype(jnp.bfloat16)
    prob_bf = prob.astype(jnp.bfloat16)
    query_grad = jnp.einsum('hqk,khd->qhd', grad_score.astype(jnp.float32), key_heads) * inv_root
    key_part = jnp.einsum('hqk,qhd->khd', grad_score.astype(jnp.float32), query_heads) * inv_root
    value_part = jnp.einsum('hqk,qhd->khd', prob_bf.astype(jnp.float32), datt_heads)
    return (query_grad.reshape(FR_DEV, HW).astype(jnp.bfloat16), key_part.reshape(LEN, HW).astype(jnp.bfloat16), value_part.reshape(LEN, HW).astype(jnp.bfloat16))

def reference(queries, attn_keys, attn_values, residual, out_weight, conv_taps, norm_gain, lengths, cotangent):
    positions = jnp.arange(LEN, dtype=jnp.int32)
    half_span = (KTAPS - 1) // 2

    def forward_utt(utter_items):
        utter_query, utter_key, utter_value, utter_length = utter_items
        key_valid = positions < utter_length
        blocks = utter_query.reshape(N_CTX, FR_DEV, HW)
        attended, log_total = lax.map(lambda query_block: forward_block(query_block, utter_key, utter_value, key_valid), blocks)
        return (attended.reshape(LEN, HW), log_total.reshape(LEN, HEADS))
    attended, log_total = lax.map(forward_utt, (queries, attn_keys, attn_values, lengths))
    projected = jnp.dot(attended.reshape(UTT * LEN, HW), out_weight, preferred_element_type=jnp.float32)
    residual_mid = (residual.astype(jnp.float32) + projected.reshape(UTT, LEN, D)).astype(jnp.bfloat16)
    mid_float = residual_mid.astype(jnp.float32)
    frame_valid = (positions[None, :] < lengths[:, None]).astype(jnp.float32)[:, :, None]
    normed = norm_part(mid_float, norm_gain, frame_valid).astype(jnp.bfloat16)
    padded = jnp.pad(normed, ((0, 0), (half_span, half_span), (0, 0)))
    conv_pre = depthwise(padded, conv_taps, LEN)
    gate_sig = jax.nn.sigmoid(conv_pre)
    layer_out = (mid_float + conv_pre * gate_sig).astype(jnp.bfloat16)
    grad_out = cotangent.astype(jnp.float32)
    grad_conv = (grad_out * gate_sig * (1.0 + conv_pre * (1.0 - gate_sig))).astype(jnp.bfloat16)
    grad_taps = tap_grads(padded, grad_conv, LEN)
    grad_padded = jnp.pad(grad_conv, ((0, 0), (half_span, half_span), (0, 0)))
    grad_normed = depthwise(grad_padded, conv_taps[::-1], LEN)
    norm_value, norm_pull = jax.vjp(lambda mid_in, gain_in: norm_part(mid_in, gain_in, frame_valid), mid_float, norm_gain)
    norm_back, grad_gain = norm_pull(grad_normed)
    grad_residual = (grad_out + norm_back).astype(jnp.bfloat16)
    att_blocks = attended.reshape(UTT * N_CTX, FR_DEV, HW)
    grad_blocks = grad_residual.reshape(UTT * N_CTX, FR_DEV, D)

    def weight_step(running, block_items):
        att_block, grad_block = block_items
        block_term = jnp.dot(att_block.T, grad_block, preferred_element_type=jnp.float32).astype(jnp.bfloat16)
        block_term = lax.optimization_barrier(block_term)
        return (running + block_term.astype(jnp.float32), None)
    grad_weight, unused = lax.scan(weight_step, jnp.zeros((HW, D), jnp.float32), (att_blocks, grad_blocks))
    grad_att = jnp.dot(grad_residual.reshape(UTT * LEN, D), out_weight.T, preferred_element_type=jnp.float32)
    grad_att = grad_att.reshape(UTT, LEN, HW).astype(jnp.bfloat16)
    row_delta = lax.optimization_barrier(jnp.sum((grad_att.astype(jnp.float32) * attended.astype(jnp.float32)).reshape(UTT, LEN, HEADS, HD), axis=3))

    def backward_utt(utter_items):
        utter_query, utter_key, utter_value, utter_length, utter_datt, utter_log, utter_delta = utter_items
        key_valid = positions < utter_length
        block_items = (utter_query.reshape(N_CTX, FR_DEV, HW), utter_datt.reshape(N_CTX, FR_DEV, HW), utter_log.reshape(N_CTX, FR_DEV, HEADS), utter_delta.reshape(N_CTX, FR_DEV, HEADS))

        def block_step(running, items_now):
            query_block, datt_block, log_block, delta_block = items_now
            query_grad, key_part, value_part = backward_block(query_block, datt_block, log_block, delta_block, utter_key, utter_value, key_valid)
            key_part, value_part = lax.optimization_barrier((key_part, value_part))
            return ((running[0] + key_part.astype(jnp.float32), running[1] + value_part.astype(jnp.float32)), query_grad)
        zero_sum = jnp.zeros((LEN, HW), jnp.float32)
        sums_out, query_grads = lax.scan(block_step, (zero_sum, zero_sum), block_items)
        return (query_grads.reshape(LEN, HW), sums_out[0].astype(jnp.bfloat16), sums_out[1].astype(jnp.bfloat16))
    grad_queries, grad_keys, grad_values = lax.map(backward_utt, (queries, attn_keys, attn_values, lengths, grad_att, log_total, row_delta))
    return (layer_out, grad_queries, grad_keys, grad_values, grad_residual, grad_weight, grad_taps, grad_gain)
```

```python
import math

import jax
import jax.numpy as jnp
from jax import lax
from jax.sharding import PartitionSpec as P

HEADS = 12
HD = 64
KTAPS = 31
HW = 768
GROUPS = 4
PER = 8
GH = HEADS // GROUPS
GW = GH * HD
HALO = 32
MASK_FILL = -1e30
NORM_EPSILON = 1e-05


def swap(block, axis, mask):
    count = lax.axis_size(axis)
    return lax.ppermute(block, axis, [(i, i ^ mask) for i in range(count)])


def bit_of(index, mask):
    return (index & mask) != 0


def by_group(blocks, group):
    first = bit_of(group, 1)
    second = bit_of(group, 2)
    low = [jnp.where(first, blocks[k ^ 1], blocks[k]) for k in range(GROUPS)]
    return [jnp.where(second, low[k ^ 2], low[k]) for k in range(GROUPS)]


def neighbours(block, width):
    count = lax.axis_size("ctx")
    forward = [(i, i + 1) for i in range(count - 1)]
    backward = [(target, source) for source, target in forward]
    low = lax.ppermute(block[block.shape[0] - width :], "ctx", forward)
    high = lax.ppermute(block[:width], "ctx", backward)
    return low, high


def norm_part(mid_float, norm_gain, frame_valid):
    row_mean = jnp.mean(mid_float, axis=-1, keepdims=True)
    centred = mid_float - row_mean
    spread = jnp.mean(centred * centred, axis=-1, keepdims=True)
    return centred * lax.rsqrt(spread + NORM_EPSILON) * norm_gain * frame_valid


def depthwise(padded, conv_taps, frames, start):
    summed = jnp.zeros((frames, padded.shape[1]), jnp.float32)
    for offset in range(KTAPS):
        summed = summed + conv_taps[offset] * padded[
            start + offset : start + offset + frames
        ].astype(jnp.float32)
    return summed


def tap_grads(padded, grad_conv, frames, start):
    rows_out = []
    for offset in range(KTAPS):
        window = padded[start + offset : start + offset + frames].astype(jnp.float32)
        rows_out.append(jnp.sum(grad_conv.astype(jnp.float32) * window, axis=0))
    return rows_out


def attention(query, pairs, bias):
    outs, logs = [], []
    for h in range(GH):
        q = query[:, h * 128 : h * 128 + HD]
        k = pairs[:, h * 128 : h * 128 + HD]
        v = pairs[:, h * 128 + HD : (h + 1) * 128]
        scores = (
            lax.dot_general(q, k, (((1,), (1,)), ((), ())), preferred_element_type=jnp.float32)
            + bias
        )
        row_max = jnp.max(scores, axis=1, keepdims=True)
        shifted = jnp.exp(scores - row_max)
        row_sum = jnp.sum(shifted, axis=1, keepdims=True)
        weights = (shifted / row_sum).astype(jnp.bfloat16)
        outs.append(jnp.dot(weights, v, preferred_element_type=jnp.float32).astype(jnp.bfloat16))
        logs.append(row_max + jnp.log(row_sum))
    return jnp.concatenate(outs, axis=1), jnp.concatenate(logs, axis=1)


def attention_back(query, pairs, bias, logs, datt, delta):
    query_grads, pair_grads = [], []
    for h in range(GH):
        q = query[:, h * 128 : h * 128 + HD]
        k = pairs[:, h * 128 : h * 128 + HD]
        v = pairs[:, h * 128 + HD : (h + 1) * 128]
        d = datt[:, h * HD : (h + 1) * HD]
        scores = (
            lax.dot_general(q, k, (((1,), (1,)), ((), ())), preferred_element_type=jnp.float32)
            + bias
        )
        prob = jnp.exp(scores - logs[:, h : h + 1])
        grad_prob = lax.dot_general(
            d, v, (((1,), (1,)), ((), ())), preferred_element_type=jnp.float32
        )
        grad_score = (prob * (grad_prob - delta[:, h : h + 1])).astype(jnp.bfloat16)
        query_grads.append(
            (jnp.dot(grad_score, k, preferred_element_type=jnp.float32) * (1.0 / 8.0)).astype(
                jnp.bfloat16
            )
        )
        contract = (((0,), (0,)), ((), ()))
        pair_grads.append(
            lax.dot_general(grad_score, q, contract, preferred_element_type=jnp.float32).astype(
                jnp.bfloat16
            )
        )
        pair_grads.append(
            lax.dot_general(
                prob.astype(jnp.bfloat16), d, contract, preferred_element_type=jnp.float32
            ).astype(jnp.bfloat16)
        )
    return jnp.concatenate(query_grads, axis=1), jnp.concatenate(pair_grads, axis=1)


def add(first, second):
    return (first.astype(jnp.float32) + second.astype(jnp.float32)).astype(first.dtype)


def halve(block, dim, axis, mask, index):
    mine = (index & mask) // mask
    kept = lax.dynamic_index_in_dim(block, mine, dim, keepdims=False)
    sent = lax.dynamic_index_in_dim(block, 1 - mine, dim, keepdims=False)
    return add(kept, swap(sent, axis, mask))


def regather(block, axis, mask, index):
    other = swap(block, axis, mask)
    high = bit_of(index, mask)
    return jnp.concatenate(
        [jnp.where(high, other, block), jnp.where(high, block, other)], axis=0
    )


def sum_everywhere(rows, ctx, dp):
    part = rows
    for mask in (1, 2, 4):
        part = part.reshape(2, part.shape[0] // 2, part.shape[1])
        part = halve(part, 0, "ctx", mask, ctx)
    for mask in (8, 16):
        part = part + swap(part, "ctx", mask)
    mask = 1
    while mask < lax.axis_size("dp"):
        part = part + swap(part, "dp", mask)
        mask *= 2
    for mask in (4, 2, 1):
        part = regather(part, "ctx", mask, ctx)
    return part


def shards(
    queries, attn_keys, attn_values, residual, out_weight, conv_taps, norm_gain, lengths, cotangent
):
    frames = queries.shape[1]
    width = residual.shape[2]
    ctx = lax.axis_index("ctx")
    dp = lax.axis_index("dp")
    dp_size = lax.axis_size("dp")
    group = ctx // PER
    member = ctx % PER
    length = lengths[0]

    weight_all = lax.all_gather(out_weight, "dp", axis=0, tiled=True)
    cot_low, cot_high = neighbours(cotangent[0], HALO // 2)

    query_scaled = (queries[0].astype(jnp.float32) * (1.0 / math.sqrt(HD))).astype(jnp.bfloat16)
    pieces = []
    for g in range(GROUPS):
        cols = []
        for h in range(GH):
            first = (g * GH + h) * HD
            cols += [attn_keys[0][:, first : first + HD], attn_values[0][:, first : first + HD]]
        cols.append(query_scaled[:, g * GW : (g + 1) * GW])
        pieces.append(jnp.concatenate(cols, axis=1))
    relative = by_group(pieces, group)
    received = [relative[0]] + [swap(relative[k], "ctx", k * PER) for k in range(1, GROUPS)]
    held = jnp.concatenate(by_group(received, group), axis=0)
    own_pairs, query = held[:, : GH * 128], held[:, GH * 128 :]
    rows = own_pairs.shape[0]
    query = jnp.pad(query.reshape(rows, GH, HD), ((0, 0), (0, 0), (0, HD))).reshape(rows, GH * 128)

    half = rows // 2
    from_x = swap(own_pairs, "ctx", 2)
    from_z = swap(own_pairs, "ctx", 4)
    diag = jnp.concatenate(
        [swap(from_z[:half], "ctx", 2), swap(from_x[half:], "ctx", 4)], axis=0
    )
    near = jnp.concatenate([own_pairs, from_x, from_z, diag], axis=0)
    pairs = jnp.concatenate([near, swap(near, "ctx", 1)], axis=0)
    order = [0, 2, 4, 6, 1, 3, 5, 7]
    starts = jnp.concatenate(
        [
            jnp.stack([(PER * g + (member ^ k)) * frames for g in range(GROUPS)])
            for k in order
        ]
    )
    positions = (starts[:, None] + jnp.arange(frames, dtype=jnp.int32)[None, :]).reshape(1, -1)
    bias = jnp.where(positions < length, 0.0, MASK_FILL).astype(jnp.float32)

    att_heads, log_total = attention(query, pairs, bias)

    def rows_home(block):
        parts = by_group([block[g * frames : (g + 1) * frames] for g in range(GROUPS)], group)
        back = [parts[0]] + [swap(parts[k], "ctx", k * PER) for k in range(1, GROUPS)]
        return by_group(back, group)

    attended = jnp.concatenate(rows_home(att_heads), axis=1)
    projected = jnp.dot(attended, weight_all, preferred_element_type=jnp.float32)
    residual_mid = (residual[0].astype(jnp.float32) + projected).astype(jnp.bfloat16)
    mid_float = residual_mid.astype(jnp.float32)
    first_frame = ctx * frames
    local_valid = first_frame + jnp.arange(frames, dtype=jnp.int32) < length
    frame_valid = local_valid.astype(jnp.float32)[:, None]
    normed = norm_part(mid_float, norm_gain, frame_valid).astype(jnp.bfloat16)
    norm_low, norm_high = neighbours(normed, HALO)
    padded = jnp.concatenate([norm_low, normed, norm_high], axis=0)
    side = HALO // 2
    cot_ext = jnp.concatenate([cot_low, cotangent[0], cot_high], axis=0).astype(jnp.float32)
    conv_ext = depthwise(padded, conv_taps, frames + HALO, 1)
    sig_ext = jax.nn.sigmoid(conv_ext)
    grad_conv_ext = (cot_ext * sig_ext * (1.0 + conv_ext * (1.0 - sig_ext))).astype(jnp.bfloat16)
    conv_pre = conv_ext[side : side + frames]
    gate_sig = sig_ext[side : side + frames]
    layer_out = (mid_float + conv_pre * gate_sig).astype(jnp.bfloat16)
    grad_out = cotangent[0].astype(jnp.float32)
    local_taps = tap_grads(padded, grad_conv_ext[side : side + frames], frames, side + 1)
    grad_normed = depthwise(grad_conv_ext, conv_taps[::-1], frames, 1)
    norm_value, norm_pull = jax.vjp(
        lambda mid_in, gain_in: norm_part(mid_in, gain_in, frame_valid), mid_float, norm_gain
    )
    norm_back, local_gain = norm_pull(grad_normed)
    summed = sum_everywhere(jnp.stack(local_taps + [local_gain]), ctx, dp)
    grad_taps, grad_gain = summed[:KTAPS], summed[KTAPS]
    grad_residual = (grad_out + norm_back).astype(jnp.bfloat16)

    grad_att = lax.dot_general(
        grad_residual, weight_all, (((1,), (1,)), ((), ())), preferred_element_type=jnp.float32
    ).astype(jnp.bfloat16)

    parts = by_group([grad_att[:, g * GW : (g + 1) * GW] for g in range(GROUPS)], group)
    arrived = [parts[0]] + [swap(parts[k], "ctx", k * PER) for k in range(1, GROUPS)]
    datt = jnp.concatenate(by_group(arrived, group), axis=0)
    delta = jnp.sum(
        (datt.astype(jnp.float32) * att_heads.astype(jnp.float32)).reshape(rows, GH, HD), axis=2
    )

    part = lax.dot_general(
        attended, grad_residual, (((0,), (0,)), ((), ())), preferred_element_type=jnp.float32
    ).astype(jnp.bfloat16)
    part = part.reshape(2, 2, 2, 2, 2, HW // 32, width)
    part = halve(part, 4, "ctx", 1, ctx)
    part = halve(part, 3, "ctx", 2, ctx)
    part = halve(part, 2, "ctx", 4, ctx)
    part = halve(part, 1, "ctx", 8, ctx)
    part = halve(part, 0, "ctx", 16, ctx)
    mask = dp_size // 2
    while mask:
        part = part.reshape(part.shape[0], 2, part.shape[1] // 2)
        part = halve(part, 1, "dp", mask, dp)
        mask //= 2
    grad_weight = part.astype(jnp.float32)

    query_grad, pair_grad = attention_back(query, pairs, bias, log_total, datt, delta)

    total = pair_grad.shape[0]
    near = add(pair_grad[: total // 2], swap(pair_grad[total // 2 :], "ctx", 1))
    own, to_x, to_z, far = [near[i * rows : (i + 1) * rows] for i in range(4)]
    far_x = swap(far[:half], "ctx", 2)
    far_z = swap(far[half:], "ctx", 4)
    to_z = jnp.concatenate([add(to_z[:half], far_x), to_z[half:]], axis=0)
    to_x = jnp.concatenate([to_x[:half], add(to_x[half:], far_z)], axis=0)
    pair_sum = (
        own.astype(jnp.float32)
        + swap(to_x, "ctx", 2).astype(jnp.float32)
        + swap(to_z, "ctx", 4).astype(jnp.float32)
    ).astype(jnp.bfloat16)
    home = rows_home(jnp.concatenate([pair_sum, query_grad], axis=1))
    keys_out, values_out, queries_out = [], [], []
    for block in home:
        for h in range(GH):
            keys_out.append(block[:, h * 128 : h * 128 + HD])
            values_out.append(block[:, h * 128 + HD : (h + 1) * 128])
        queries_out.append(block[:, GH * 128 :])
    return (
        layer_out[None],
        jnp.concatenate(queries_out, axis=1)[None],
        jnp.concatenate(keys_out, axis=1)[None],
        jnp.concatenate(values_out, axis=1)[None],
        grad_residual[None],
        grad_weight,
        grad_taps,
        grad_gain,
    )


def solution(mesh):
    placed = (
        P("dp", "ctx", None),
        P("dp", "ctx", None),
        P("dp", "ctx", None),
        P("dp", "ctx", None),
        P("dp", None),
        P(),
        P(),
        P("dp"),
        P("dp", "ctx", None),
    )
    return jax.shard_map(
        shards,
        mesh=mesh,
        in_specs=placed,
        out_specs=(
            P("dp", "ctx", None),
            P("dp", "ctx", None),
            P("dp", "ctx", None),
            P("dp", "ctx", None),
            P("dp", "ctx", None),
            P("ctx", "dp"),
            P(),
            P(),
        ),
        check_vma=False,
    )
```

```python
import functools
import math

import jax
import jax.numpy as jnp
from jax import lax
from jax.experimental import pallas as pl
from jax.experimental.pallas import tpu as pltpu
from jax.sharding import PartitionSpec as P

HEADS = 12
HD = 64
KTAPS = 31
HW = 768
GROUPS = 4
PER = 8
GH = HEADS // GROUPS
GW = GH * HD
HALO = 32
MASK_FILL = -1e30
NORM_EPSILON = 1e-05
VMEM = 48 << 20
NT = (((1,), (1,)), ((), ()))


def swap(block, axis, mask):
    count = lax.axis_size(axis)
    return lax.ppermute(block, axis, [(i, i ^ mask) for i in range(count)])


def bit_of(index, mask):
    return (index & mask) != 0


def by_group(blocks, group):
    first = bit_of(group, 1)
    second = bit_of(group, 2)
    low = [jnp.where(first, blocks[k ^ 1], blocks[k]) for k in range(GROUPS)]
    return [jnp.where(second, low[k ^ 2], low[k]) for k in range(GROUPS)]


def neighbours(first, last):
    count = lax.axis_size("ctx")
    forward = [(i, i + 1) for i in range(count - 1)]
    backward = [(target, source) for source, target in forward]
    return lax.ppermute(last, "ctx", forward), lax.ppermute(first, "ctx", backward)


def norm_part(mid_float, norm_gain, frame_valid):
    row_mean = jnp.mean(mid_float, axis=-1, keepdims=True)
    centred = mid_float - row_mean
    spread = jnp.mean(centred * centred, axis=-1, keepdims=True)
    return centred * lax.rsqrt(spread + NORM_EPSILON) * norm_gain * frame_valid


def depthwise(padded, conv_taps, frames, start):
    summed = jnp.zeros((frames, padded.shape[1]), jnp.float32)
    for offset in range(KTAPS):
        summed = summed + conv_taps[offset] * padded[
            start + offset : start + offset + frames
        ].astype(jnp.float32)
    return summed


def tap_grads(padded, grad_conv, frames, start):
    rows_out = []
    for offset in range(KTAPS):
        window = padded[start + offset : start + offset + frames].astype(jnp.float32)
        rows_out.append(jnp.sum(grad_conv.astype(jnp.float32) * window, axis=0))
    return rows_out


def lanes_of(shape):
    return lax.broadcasted_iota(jnp.int32, shape, 1)


def rows_of(refs):
    return refs[0][...] if len(refs) == 1 else jnp.concatenate([ref[...] for ref in refs], axis=0)


def forward_kernel(count, merge, *refs):
    q_ref, kv_refs, bias_ref = refs[0], refs[1 : 1 + count], refs[1 + count]
    kv = rows_of(kv_refs)
    lane = lanes_of(kv.shape)
    k_aug = jnp.where(lane < HD, kv, bias_ref[...])
    v_aug = jnp.where(lane < HD, jnp.ones_like(kv), kv)
    scores = lax.dot_general(q_ref[...], k_aug, NT, preferred_element_type=jnp.float32)
    row_max = jnp.max(scores, axis=1, keepdims=True)
    weights = jnp.exp(scores - row_max).astype(jnp.bfloat16)
    acc = jnp.dot(weights, v_aug, preferred_element_type=jnp.float32)
    total = pltpu.roll(acc, HD, 1)
    low = lanes_of(acc.shape) < HD
    out = jnp.where(low, row_max + jnp.log(acc), acc / total)
    if not merge:
        refs[-1][...] = out
        return
    prev_ref, att_ref, log_ref = refs[2 + count :]
    prev = prev_ref[...]
    mine = jnp.where(low, out, pltpu.roll(out, HD, 1))
    theirs = jnp.where(low, prev, pltpu.roll(prev, HD, 1))
    top = jnp.maximum(mine, theirs)
    both = top + jnp.log(jnp.exp(mine - top) + jnp.exp(theirs - top))
    att_ref[...] = (out * jnp.exp(mine - both) + prev * jnp.exp(theirs - both)).astype(jnp.bfloat16)
    log_ref[0] = jnp.transpose(both)[:8]


def attention(query, pieces, bias, half, prev=None, block=256):
    n, keys = query.shape[0], bias.shape[0] // 2
    row = pl.BlockSpec((block, 128), lambda h, i: (i, h))
    ins = [row]
    ins += [pl.BlockSpec((piece.shape[0], 128), lambda h, i: (0, h)) for piece in pieces]
    ins.append(pl.BlockSpec((keys, 128), lambda h, i: (half, 0)))
    args = [query, *pieces, bias]
    out_specs, out_shape = row, jax.ShapeDtypeStruct((n, GH * 128), jnp.float32)
    if prev is not None:
        ins.append(row)
        args.append(prev)
        out_specs = [row, pl.BlockSpec((1, 8, block), lambda h, i: (h, 0, i))]
        out_shape = [
            jax.ShapeDtypeStruct((n, GH * 128), jnp.bfloat16),
            jax.ShapeDtypeStruct((GH, 8, n), jnp.float32),
        ]
    return pl.pallas_call(
        functools.partial(forward_kernel, len(pieces), prev is not None),
        grid=(GH, n // block),
        in_specs=ins,
        out_specs=out_specs,
        out_shape=out_shape,
        cost_estimate=pl.CostEstimate(
            flops=8 * n * keys * GH * 128, bytes_accessed=1 << 22, transcendentals=n * keys * GH
        ),
        compiler_params=pltpu.CompilerParams(vmem_limit_bytes=VMEM),
    )(*args)


def backward_kernel(count, splits, last, *refs):
    q_ref, do_ref, att_ref, log_ref = refs[:4]
    kv_refs, bias_ref = refs[4 : 4 + count], refs[4 + count]
    outs = refs[5 + count :]
    q = q_ref[...]
    q_only = jnp.where(lanes_of(q.shape) < HD, q, jnp.zeros_like(q))
    do = do_ref[...]
    log_row = log_ref[0, 0:1, :]
    products = do.astype(jnp.float32) * att_ref[...].astype(jnp.float32)
    delta = jnp.sum(jnp.transpose(products), axis=0, keepdims=True)
    kv_all = rows_of(kv_refs)
    bias_all = bias_ref[...]
    grads, dq = [], None
    step = kv_all.shape[0] // 2
    for part in range(2):
        kv = kv_all[part * step : (part + 1) * step]
        bias = bias_all[part * step : (part + 1) * step]
        k_aug = jnp.where(lanes_of(kv.shape) < HD, kv, bias)
        scores = lax.dot_general(k_aug, q, NT, preferred_element_type=jnp.float32)
        prob = jnp.exp(scores - log_row)
        grad_prob = lax.dot_general(kv, do, NT, preferred_element_type=jnp.float32)
        grad_score = (prob * (grad_prob - delta)).astype(jnp.bfloat16)
        grads.append(
            (
                jnp.dot(grad_score, q_only, preferred_element_type=jnp.float32)
                + jnp.dot(prob.astype(jnp.bfloat16), do, preferred_element_type=jnp.float32)
            ).astype(jnp.bfloat16)
        )
        term = jnp.dot(jnp.transpose(kv), grad_score, preferred_element_type=jnp.float32)
        dq = term if dq is None else dq + term
    at = 0
    flat = jnp.concatenate(grads, axis=0)
    for ref in outs[1 + last :]:
        ref[...] = flat[at : at + ref.shape[0]]
        at += ref.shape[0]
    if last:
        outs[1][...] = (jnp.transpose(dq + outs[0][0]) * (1.0 / math.sqrt(HD))).astype(jnp.bfloat16)
    else:
        outs[0][0] = dq


def attention_back(query, datt, att, log, pieces, bias, half, splits, prev=None):
    n, keys = query.shape[0], bias.shape[0] // 2
    full = pl.BlockSpec((n, 128), lambda h: (0, h))
    cols = pl.BlockSpec((1, 128, n), lambda h: (h, 0, 0))
    ins = [full, full, full, pl.BlockSpec((1, 8, n), lambda h: (h, 0, 0))]
    ins += [pl.BlockSpec((piece.shape[0], 128), lambda h: (0, h)) for piece in pieces]
    ins.append(pl.BlockSpec((keys, 128), lambda h: (half, 0)))
    args = [query, datt, att, log, *pieces, bias]
    if prev is None:
        outs, shapes = [cols], [jax.ShapeDtypeStruct((GH, 128, n), jnp.float32)]
    else:
        ins.append(cols)
        args.append(prev)
        outs, shapes = [full], [jax.ShapeDtypeStruct((n, GH * 128), jnp.bfloat16)]
    outs += [pl.BlockSpec((size, 128), lambda h: (0, h)) for size in splits]
    shapes += [jax.ShapeDtypeStruct((size, GH * 128), jnp.bfloat16) for size in splits]
    return pl.pallas_call(
        functools.partial(backward_kernel, len(pieces), splits, prev is not None),
        grid=(GH,),
        in_specs=ins,
        out_specs=outs,
        out_shape=shapes,
        cost_estimate=pl.CostEstimate(
            flops=20 * n * keys * GH * 128, bytes_accessed=1 << 22, transcendentals=n * keys * GH
        ),
        compiler_params=pltpu.CompilerParams(vmem_limit_bytes=VMEM),
    )(*args)


def add(first, second):
    return (first.astype(jnp.float32) + second.astype(jnp.float32)).astype(first.dtype)


def pick(block, dim, mask, index):
    mine = (index & mask) // mask
    kept = lax.dynamic_index_in_dim(block, mine, dim, keepdims=False)
    sent = lax.dynamic_index_in_dim(block, 1 - mine, dim, keepdims=False)
    return kept, sent


def gradient_sums(part, rows, ctx):
    count = rows.shape[0]
    width = rows.shape[1]
    for dim, mask in ((3, 2), (2, 4), (1, 8), (0, 16)):
        kept, sent = pick(part, dim, mask, ctx)
        rows = rows.astype(jnp.bfloat16)
        other = swap(
            jnp.concatenate([sent.reshape(-1, width), rows], axis=0), "ctx", mask
        )
        part = add(kept, other[:-count].reshape(kept.shape))
        rows = rows.astype(jnp.float32) + other[-count:].astype(jnp.float32)
    mask = 1
    while mask < lax.axis_size("dp"):
        joined = jnp.concatenate([part, rows.astype(jnp.bfloat16)], axis=0)
        other = swap(joined, "dp", mask)
        summed = joined.astype(jnp.float32) + other.astype(jnp.float32)
        part, rows = summed[:-count].astype(jnp.bfloat16), summed[-count:]
        mask *= 2
    return summed[:-count], rows


def shards(
    queries, attn_keys, attn_values, residual, out_weight, conv_taps, norm_gain, lengths, cotangent
):
    frames = queries.shape[1]
    width = residual.shape[2]
    ctx = lax.axis_index("ctx")
    dp = lax.axis_index("dp")
    dp_size = lax.axis_size("dp")
    group = ctx // PER
    member = ctx % PER
    length = lengths[0]

    core = ctx % 2
    owned = out_weight.shape[0] // 2
    weight_half = lax.all_gather(
        lax.dynamic_slice_in_dim(out_weight, core * owned, owned, 0), "dp", axis=0
    )
    weight_other = swap(weight_half, "ctx", 1)
    odd = core == 1
    weight_all = jnp.stack(
        [jnp.where(odd, weight_other, weight_half), jnp.where(odd, weight_half, weight_other)],
        axis=1,
    ).reshape(HW, width)

    query_scaled = (queries[0].astype(jnp.float32) * (1.0 / math.sqrt(HD))).astype(jnp.bfloat16)
    pieces = []
    for g in range(GROUPS):
        cols = []
        for h in range(GH):
            first = (g * GH + h) * HD
            cols += [attn_keys[0][:, first : first + HD], attn_values[0][:, first : first + HD]]
        cols.append(query_scaled[:, g * GW : (g + 1) * GW])
        pieces.append(jnp.concatenate(cols, axis=1))
    relative = by_group(pieces, group)
    received = [relative[0]] + [swap(relative[k], "ctx", k * PER) for k in range(1, GROUPS)]
    held = jnp.concatenate(by_group(received, group), axis=0)
    own_pairs, query = held[:, : GH * 128], held[:, GH * 128 :]
    rows = own_pairs.shape[0]
    one = (jnp.arange(HD) == 0).astype(jnp.bfloat16)
    query = jnp.concatenate(
        [query.reshape(rows, GH, HD), jnp.broadcast_to(one, (rows, GH, HD))], axis=2
    ).reshape(rows, GH * 128)

    half = rows // 2
    core_own = swap(own_pairs, "ctx", 1)
    from_x = swap(own_pairs, "ctx", 2)
    from_z = swap(own_pairs, "ctx", 4)
    diag_low = swap(from_z[:half], "ctx", 2)
    diag_high = swap(from_x[half:], "ctx", 4)
    near = [own_pairs, from_x, from_z, diag_low, diag_high]
    far = [core_own, swap(jnp.concatenate(near[1:], axis=0), "ctx", 1)]
    order = [0, 2, 4, 6, 1, 3, 5, 7]
    starts = jnp.concatenate(
        [
            jnp.stack([(PER * g + (member ^ k)) * frames for g in range(GROUPS)])
            for k in order
        ]
    )
    positions = (starts[:, None] + jnp.arange(frames, dtype=jnp.int32)[None, :]).reshape(-1, 1)
    masked = (positions >= length) & (jnp.arange(2 * HD) == HD)[None, :]
    bias = jnp.where(masked, MASK_FILL, 0.0).astype(jnp.bfloat16)

    first_half = attention(query, near, bias, 0)
    att_wide, log_total = attention(query, far, bias, 1, first_half)
    att_heads = att_wide.reshape(rows, GH, 2, HD)[:, :, 1].reshape(rows, GW)

    def rows_home(block):
        parts = by_group([block[g * frames : (g + 1) * frames] for g in range(GROUPS)], group)
        back = [parts[0]] + [swap(parts[k], "ctx", k * PER) for k in range(1, GROUPS)]
        return by_group(back, group)

    attended = jnp.concatenate(rows_home(att_heads), axis=1)
    projected = jnp.dot(attended, weight_all, preferred_element_type=jnp.float32)
    residual_mid = (residual[0].astype(jnp.float32) + projected).astype(jnp.bfloat16)
    mid_float = residual_mid.astype(jnp.float32)
    first_frame = ctx * frames
    local_valid = first_frame + jnp.arange(frames, dtype=jnp.int32) < length
    frame_valid = local_valid.astype(jnp.float32)[:, None]
    normed = norm_part(mid_float, norm_gain, frame_valid).astype(jnp.bfloat16)
    side = HALO // 2
    cot = cotangent[0]
    low, high = neighbours(
        jnp.concatenate([normed[:HALO], cot[:side]], axis=0),
        jnp.concatenate([normed[frames - HALO :], cot[frames - side :]], axis=0),
    )
    padded = jnp.concatenate([low[:HALO], normed, high[:HALO]], axis=0)
    cot_low, cot_high = low[HALO:], high[HALO:]
    cot_ext = jnp.concatenate([cot_low, cotangent[0], cot_high], axis=0).astype(jnp.float32)
    conv_ext = depthwise(padded, conv_taps, frames + HALO, 1)
    sig_ext = jax.nn.sigmoid(conv_ext)
    grad_conv_ext = (cot_ext * sig_ext * (1.0 + conv_ext * (1.0 - sig_ext))).astype(jnp.bfloat16)
    conv_pre = conv_ext[side : side + frames]
    gate_sig = sig_ext[side : side + frames]
    layer_out = (mid_float + conv_pre * gate_sig).astype(jnp.bfloat16)
    grad_out = cotangent[0].astype(jnp.float32)
    local_taps = tap_grads(padded, grad_conv_ext[side : side + frames], frames, side + 1)
    grad_normed = depthwise(grad_conv_ext, conv_taps[::-1], frames, 1)
    norm_value, norm_pull = jax.vjp(
        lambda mid_in, gain_in: norm_part(mid_in, gain_in, frame_valid), mid_float, norm_gain
    )
    norm_back, local_gain = norm_pull(grad_normed)
    grad_residual = (grad_out + norm_back).astype(jnp.bfloat16)

    grad_att = lax.dot_general(
        grad_residual, weight_all, (((1,), (1,)), ((), ())), preferred_element_type=jnp.float32
    ).astype(jnp.bfloat16)

    parts = by_group([grad_att[:, g * GW : (g + 1) * GW] for g in range(GROUPS)], group)
    moved = [parts[0]] + [swap(parts[k], "ctx", k * PER) for k in range(1, GROUPS)]
    datt = jnp.concatenate(by_group(moved, group), axis=0)
    datt_wide = jnp.pad(
        datt.reshape(rows, GH, HD), ((0, 0), (0, 0), (HD, 0))
    ).reshape(rows, GH * 128)

    pair_core = swap(jnp.concatenate([attended, grad_residual], axis=1), "ctx", 1)
    part = lax.dot_general(
        jnp.concatenate([attended, pair_core[:, :HW]], axis=0),
        jnp.concatenate([grad_residual, pair_core[:, HW:]], axis=0),
        (((0,), (0,)), ((), ())),
        preferred_element_type=jnp.float32,
    )
    part = lax.dynamic_index_in_dim(
        part.reshape(2, 2, 2, 2, 2, HW // 32, width), core, 4, keepdims=False
    ).astype(jnp.bfloat16)
    tap_rows = jnp.stack(local_taps + [local_gain]).astype(jnp.bfloat16)
    tap_rows = tap_rows.astype(jnp.float32) + swap(tap_rows, "ctx", 1).astype(jnp.float32)
    weight_sum, tap_sum = gradient_sums(part, tap_rows, ctx)
    grad_weight = lax.dynamic_slice_in_dim(weight_sum, dp * (width // dp_size), width // dp_size, 1)
    grad_taps, grad_gain = tap_sum[:KTAPS], tap_sum[KTAPS]

    query_half, far_grad = attention_back(
        query, datt_wide, att_wide, log_total, far, bias, 1, (4 * rows,)
    )
    arrived = swap(far_grad, "ctx", 1)
    query_wide, own, to_x, to_z, far_low, far_high = attention_back(
        query, datt_wide, att_wide, log_total, near, bias, 0,
        (rows, rows, rows, half, half), query_half,
    )
    query_grad = query_wide.reshape(rows, GH, 2, HD)[:, :, 0].reshape(rows, GW)
    far_x = swap(add(far_low, arrived[3 * rows : 3 * rows + half]), "ctx", 2)
    far_z = swap(add(far_high, arrived[3 * rows + half :]), "ctx", 4)
    to_x = to_x.astype(jnp.float32) + arrived[rows : 2 * rows].astype(jnp.float32)
    to_z = to_z.astype(jnp.float32) + arrived[2 * rows : 3 * rows].astype(jnp.float32)
    to_z = jnp.concatenate([to_z[:half] + far_x.astype(jnp.float32), to_z[half:]], axis=0)
    to_x = jnp.concatenate([to_x[:half], to_x[half:] + far_z.astype(jnp.float32)], axis=0)
    pair_sum = (
        own.astype(jnp.float32)
        + arrived[:rows].astype(jnp.float32)
        + swap(to_x.astype(jnp.bfloat16), "ctx", 2).astype(jnp.float32)
        + swap(to_z.astype(jnp.bfloat16), "ctx", 4).astype(jnp.float32)
    ).astype(jnp.bfloat16)
    home = rows_home(jnp.concatenate([pair_sum, query_grad], axis=1))
    keys_out, values_out, queries_out = [], [], []
    for block in home:
        for h in range(GH):
            keys_out.append(block[:, h * 128 : h * 128 + HD])
            values_out.append(block[:, h * 128 + HD : (h + 1) * 128])
        queries_out.append(block[:, GH * 128 :])
    return (
        layer_out[None],
        jnp.concatenate(queries_out, axis=1)[None],
        jnp.concatenate(keys_out, axis=1)[None],
        jnp.concatenate(values_out, axis=1)[None],
        grad_residual[None],
        grad_weight,
        grad_taps,
        grad_gain,
    )


def solution(mesh):
    placed = (
        P("dp", "ctx", None),
        P("dp", "ctx", None),
        P("dp", "ctx", None),
        P("dp", "ctx", None),
        P("dp", None),
        P(),
        P(),
        P("dp"),
        P("dp", "ctx", None),
    )
    return jax.shard_map(
        shards,
        mesh=mesh,
        in_specs=placed,
        out_specs=(
            P("dp", "ctx", None),
            P("dp", "ctx", None),
            P("dp", "ctx", None),
            P("dp", "ctx", None),
            P("dp", "ctx", None),
            P("ctx", "dp"),
            P(),
            P(),
        ),
        check_vma=False,
    )
```

```python
import functools
import math

import jax
import jax.numpy as jnp
from jax import lax
from jax.experimental import pallas as pl
from jax.experimental.pallas import tpu as pltpu
from jax.sharding import PartitionSpec as P

HEADS = 12
HD = 64
KTAPS = 31
HW = 768
GROUPS = 4
PER = 8
GH = HEADS // GROUPS
GW = GH * HD
HALO = 32
MASK_FILL = -1e30
NORM_EPSILON = 1e-05
VMEM = 48 << 20
NT = (((1,), (1,)), ((), ()))


def swap(block, axis, mask):
    count = lax.axis_size(axis)
    return lax.ppermute(block, axis, [(i, i ^ mask) for i in range(count)])


def bit_of(index, mask):
    return (index & mask) != 0


def by_group(blocks, group):
    first = bit_of(group, 1)
    second = bit_of(group, 2)
    low = [jnp.where(first, blocks[k ^ 1], blocks[k]) for k in range(GROUPS)]
    return [jnp.where(second, low[k ^ 2], low[k]) for k in range(GROUPS)]


def neighbours(first, last):
    count = lax.axis_size("ctx")
    forward = [(i, i + 1) for i in range(count - 1)]
    backward = [(target, source) for source, target in forward]
    return lax.ppermute(last, "ctx", forward), lax.ppermute(first, "ctx", backward)


def norm_part(mid_float, norm_gain, frame_valid):
    row_mean = jnp.mean(mid_float, axis=-1, keepdims=True)
    centred = mid_float - row_mean
    spread = jnp.mean(centred * centred, axis=-1, keepdims=True)
    return centred * lax.rsqrt(spread + NORM_EPSILON) * norm_gain * frame_valid


def conv_kernel(
    valid_ref, normed_ref, low_ref, high_ref, mid_ref, cot_ref, mid_all, cot_all, taps_ref,
    out_ref, grad_ref, rows_ref, frames_buf, conv_buf, mean_buf, scale_buf, back_buf, sum_buf, dot_buf
):
    step = pl.program_id(0)
    frames, width = mid_all.shape
    side = HALO // 2
    f32 = jnp.float32

    @pl.when(step == 0)
    def _():
        mid = mid_all[...].astype(f32)
        mean = jnp.mean(mid, axis=1, keepdims=True)
        centred = mid - mean
        scale = lax.rsqrt(jnp.mean(centred * centred, axis=1, keepdims=True) + NORM_EPSILON)
        mean_buf[...] = jnp.broadcast_to(mean, mean_buf.shape)
        scale_buf[...] = jnp.broadcast_to(scale, scale_buf.shape)
        sum_buf[...] = jnp.zeros_like(sum_buf)
        dot_buf[...] = jnp.zeros_like(dot_buf)

    frames_buf[:HALO] = low_ref[:HALO].astype(f32)
    frames_buf[HALO : HALO + frames] = normed_ref[...].astype(f32)
    frames_buf[HALO + frames :] = high_ref[:HALO].astype(f32)
    conv = jnp.zeros((frames + HALO, 128), f32)
    for k in range(KTAPS):
        conv = conv + taps_ref[k : k + 1, :] * frames_buf[1 + k : 1 + k + frames + HALO, :]
    sig = jax.nn.sigmoid(conv)
    cot = jnp.concatenate([low_ref[HALO:], cot_ref[...], high_ref[HALO:]], axis=0).astype(f32)
    grad_conv = (cot * sig * (1.0 + conv * (1.0 - sig))).astype(jnp.bfloat16).astype(f32)
    conv_buf[...] = grad_conv
    mid = mid_ref[...].astype(f32)
    out_ref[...] = (mid + (conv * sig)[side : side + frames]).astype(jnp.bfloat16)
    own = grad_conv[side : side + frames]
    rows = []
    for k in range(KTAPS):
        window = frames_buf[side + 1 + k : side + 1 + k + frames, :]
        rows.append(jnp.sum(own * window, axis=0, keepdims=True))
    back = jnp.zeros((frames, 128), f32)
    for k in range(KTAPS):
        last = KTAPS - 1 - k
        back = back + taps_ref[last : last + 1, :] * conv_buf[1 + k : 1 + k + frames, :]
    valid = lax.broadcasted_iota(jnp.int32, (frames, 128), 0) < valid_ref[0]
    back = jnp.where(valid, back, 0.0)
    unit = (mid - mean_buf[...]) * scale_buf[...]
    rows.append(jnp.sum(back * unit, axis=0, keepdims=True))
    rows_ref[...] = jnp.concatenate(rows, axis=0).astype(jnp.bfloat16)
    back = back * taps_ref[KTAPS : KTAPS + 1, :]
    back_buf[step] = back
    sum_buf[...] += back
    dot_buf[...] += back * unit

    @pl.when(step == pl.num_programs(0) - 1)
    def _():
        shift = jnp.mean(sum_buf[...], axis=1, keepdims=True) * (128.0 / width)
        slope = jnp.mean(dot_buf[...], axis=1, keepdims=True) * (128.0 / width)
        for c in range(width // 128):
            at = slice(c * 128, (c + 1) * 128)
            unit = (mid_all[:, at].astype(f32) - mean_buf[...]) * scale_buf[...]
            grad = scale_buf[...] * (back_buf[c] - shift - unit * slope)
            grad_ref[:, at] = (cot_all[:, at].astype(f32) + grad).astype(jnp.bfloat16)


def conv_part(valid_count, normed, low, high, mid, cot, taps):
    frames, width = mid.shape
    block = pl.BlockSpec((frames, 128), lambda c: (0, c))
    edge = pl.BlockSpec((low.shape[0], 128), lambda c: (0, c))
    whole = pl.BlockSpec((frames, width), lambda c: (0, 0))
    tap = pl.BlockSpec((KTAPS + 1, 128), lambda c: (0, c))
    square = pltpu.VMEM((frames, 128), jnp.float32)
    return pl.pallas_call(
        conv_kernel,
        grid=(width // 128,),
        in_specs=[
            pl.BlockSpec(memory_space=pltpu.SMEM), block, edge, edge, block, block, whole, whole, tap,
        ],
        out_specs=[block, whole, tap],
        out_shape=[
            jax.ShapeDtypeStruct((frames, width), jnp.bfloat16),
            jax.ShapeDtypeStruct((frames, width), jnp.bfloat16),
            jax.ShapeDtypeStruct((KTAPS + 1, width), jnp.bfloat16),
        ],
        scratch_shapes=[
            pltpu.VMEM((frames + 2 * HALO, 128), jnp.float32),
            pltpu.VMEM((frames + HALO, 128), jnp.float32),
            square,
            square,
            pltpu.VMEM((width // 128, frames, 128), jnp.float32),
            square,
            square,
        ],
        cost_estimate=pl.CostEstimate(
            flops=200 * frames * width, bytes_accessed=1 << 22, transcendentals=frames * width
        ),
        compiler_params=pltpu.CompilerParams(vmem_limit_bytes=VMEM),
    )(valid_count, normed, low, high, mid, cot, mid, cot, taps)


def lanes_of(shape):
    return lax.broadcasted_iota(jnp.int32, shape, 1)


def rows_of(refs):
    return refs[0][...] if len(refs) == 1 else jnp.concatenate([ref[...] for ref in refs], axis=0)


def forward_kernel(count, merge, *refs):
    q_ref, kv_refs, bias_ref = refs[0], refs[1 : 1 + count], refs[1 + count]
    kv = rows_of(kv_refs)
    lane = lanes_of(kv.shape)
    k_aug = jnp.where(lane < HD, kv, bias_ref[...])
    v_aug = jnp.where(lane < HD, jnp.ones_like(kv), kv)
    scores = lax.dot_general(q_ref[...], k_aug, NT, preferred_element_type=jnp.float32)
    row_max = jnp.max(scores, axis=1, keepdims=True)
    weights = jnp.exp(scores - row_max).astype(jnp.bfloat16)
    acc = jnp.dot(weights, v_aug, preferred_element_type=jnp.float32)
    total = pltpu.roll(acc, HD, 1)
    low = lanes_of(acc.shape) < HD
    out = jnp.where(low, row_max + jnp.log(acc), acc / total)
    if not merge:
        refs[-1][...] = out
        return
    prev_ref, att_ref, log_ref = refs[2 + count :]
    prev = prev_ref[...]
    mine = jnp.where(low, out, pltpu.roll(out, HD, 1))
    theirs = jnp.where(low, prev, pltpu.roll(prev, HD, 1))
    top = jnp.maximum(mine, theirs)
    both = top + jnp.log(jnp.exp(mine - top) + jnp.exp(theirs - top))
    att_ref[...] = (out * jnp.exp(mine - both) + prev * jnp.exp(theirs - both)).astype(jnp.bfloat16)
    log_ref[0] = jnp.transpose(both)[:8]


def attention(query, pieces, bias, half, prev=None, block=256):
    n, keys = query.shape[0], bias.shape[0] // 2
    row = pl.BlockSpec((block, 128), lambda h, i: (i, h))
    ins = [row]
    ins += [pl.BlockSpec((piece.shape[0], 128), lambda h, i: (0, h)) for piece in pieces]
    ins.append(pl.BlockSpec((keys, 128), lambda h, i: (half, 0)))
    args = [query, *pieces, bias]
    out_specs, out_shape = row, jax.ShapeDtypeStruct((n, GH * 128), jnp.float32)
    if prev is not None:
        ins.append(row)
        args.append(prev)
        out_specs = [row, pl.BlockSpec((1, 8, block), lambda h, i: (h, 0, i))]
        out_shape = [
            jax.ShapeDtypeStruct((n, GH * 128), jnp.bfloat16),
            jax.ShapeDtypeStruct((GH, 8, n), jnp.float32),
        ]
    return pl.pallas_call(
        functools.partial(forward_kernel, len(pieces), prev is not None),
        grid=(GH, n // block),
        in_specs=ins,
        out_specs=out_specs,
        out_shape=out_shape,
        cost_estimate=pl.CostEstimate(
            flops=8 * n * keys * GH * 128, bytes_accessed=1 << 22, transcendentals=n * keys * GH
        ),
        compiler_params=pltpu.CompilerParams(vmem_limit_bytes=VMEM),
    )(*args)


def backward_kernel(count, splits, last, *refs):
    q_ref, do_ref, att_ref, log_ref = refs[:4]
    kv_refs, bias_ref = refs[4 : 4 + count], refs[4 + count]
    outs = refs[5 + count :]
    q = q_ref[...]
    q_only = jnp.where(lanes_of(q.shape) < HD, q, jnp.zeros_like(q))
    do = do_ref[...]
    log_row = log_ref[0, 0:1, :]
    products = do.astype(jnp.float32) * att_ref[...].astype(jnp.float32)
    delta = jnp.sum(jnp.transpose(products), axis=0, keepdims=True)
    kv_all = rows_of(kv_refs)
    bias_all = bias_ref[...]
    grads, dq = [], None
    step = kv_all.shape[0] // 2
    for part in range(2):
        kv = kv_all[part * step : (part + 1) * step]
        bias = bias_all[part * step : (part + 1) * step]
        k_aug = jnp.where(lanes_of(kv.shape) < HD, kv, bias)
        scores = lax.dot_general(k_aug, q, NT, preferred_element_type=jnp.float32)
        prob = jnp.exp(scores - log_row)
        grad_prob = lax.dot_general(kv, do, NT, preferred_element_type=jnp.float32)
        grad_score = (prob * (grad_prob - delta)).astype(jnp.bfloat16)
        grads.append(
            (
                jnp.dot(grad_score, q_only, preferred_element_type=jnp.float32)
                + jnp.dot(prob.astype(jnp.bfloat16), do, preferred_element_type=jnp.float32)
            ).astype(jnp.bfloat16)
        )
        term = jnp.dot(jnp.transpose(kv), grad_score, preferred_element_type=jnp.float32)
        dq = term if dq is None else dq + term
    at = 0
    flat = jnp.concatenate(grads, axis=0)
    for ref in outs[1 + last :]:
        ref[...] = flat[at : at + ref.shape[0]]
        at += ref.shape[0]
    if last:
        outs[1][...] = (jnp.transpose(dq + outs[0][0]) * (1.0 / math.sqrt(HD))).astype(jnp.bfloat16)
    else:
        outs[0][0] = dq


def attention_back(query, datt, att, log, pieces, bias, half, splits, prev=None):
    n, keys = query.shape[0], bias.shape[0] // 2
    full = pl.BlockSpec((n, 128), lambda h: (0, h))
    cols = pl.BlockSpec((1, 128, n), lambda h: (h, 0, 0))
    ins = [full, full, full, pl.BlockSpec((1, 8, n), lambda h: (h, 0, 0))]
    ins += [pl.BlockSpec((piece.shape[0], 128), lambda h: (0, h)) for piece in pieces]
    ins.append(pl.BlockSpec((keys, 128), lambda h: (half, 0)))
    args = [query, datt, att, log, *pieces, bias]
    if prev is None:
        outs, shapes = [cols], [jax.ShapeDtypeStruct((GH, 128, n), jnp.float32)]
    else:
        ins.append(cols)
        args.append(prev)
        outs, shapes = [full], [jax.ShapeDtypeStruct((n, GH * 128), jnp.bfloat16)]
    outs += [pl.BlockSpec((size, 128), lambda h: (0, h)) for size in splits]
    shapes += [jax.ShapeDtypeStruct((size, GH * 128), jnp.bfloat16) for size in splits]
    return pl.pallas_call(
        functools.partial(backward_kernel, len(pieces), splits, prev is not None),
        grid=(GH,),
        in_specs=ins,
        out_specs=outs,
        out_shape=shapes,
        cost_estimate=pl.CostEstimate(
            flops=20 * n * keys * GH * 128, bytes_accessed=1 << 22, transcendentals=n * keys * GH
        ),
        compiler_params=pltpu.CompilerParams(vmem_limit_bytes=VMEM),
    )(*args)


def add(first, second):
    return (first.astype(jnp.float32) + second.astype(jnp.float32)).astype(first.dtype)


def pick(block, dim, mask, index):
    mine = (index & mask) // mask
    kept = lax.dynamic_index_in_dim(block, mine, dim, keepdims=False)
    sent = lax.dynamic_index_in_dim(block, 1 - mine, dim, keepdims=False)
    return kept, sent


def over_columns(part, rows, ctx, dp):
    count = rows.shape[0]
    quarter = rows.shape[1] // 4
    joined = jnp.concatenate([part, rows.astype(jnp.bfloat16)], axis=0)
    along = dp // 2
    blocks = by_group([joined[:, j * quarter : (j + 1) * quarter] for j in range(4)], along)
    total = blocks[0].astype(jnp.float32)
    for k in range(1, 4):
        total = total + swap(blocks[k], "dp", 2 * k).astype(jnp.float32)
    rows = total[-count:]
    part = total[:-count].astype(jnp.bfloat16).reshape(2, 2, 2, 2, -1, quarter)
    for dim, mask in ((3, 2), (2, 4), (1, 8), (0, 16)):
        kept, sent = pick(part, dim, mask, ctx)
        rows = rows.astype(jnp.bfloat16)
        other = swap(jnp.concatenate([sent.reshape(-1, quarter), rows], axis=0), "ctx", mask)
        part = add(kept, other[:-count].reshape(kept.shape))
        rows = rows.astype(jnp.float32) + other[-count:].astype(jnp.float32)
    joined = jnp.concatenate([part, rows.astype(jnp.bfloat16)], axis=0)
    total = joined.astype(jnp.float32) + swap(joined, "dp", 1).astype(jnp.float32)
    half = quarter // 2
    weight = jnp.where(bit_of(dp, 1), total[:-count, half:], total[:-count, :half])
    rows = total[-count:]
    spread = [rows] + [swap(rows, "dp", 2 * k) for k in range(1, 4)]
    return weight, jnp.concatenate(by_group(spread, along), axis=1)


def shards(
    queries, attn_keys, attn_values, residual, out_weight, conv_taps, norm_gain, lengths, cotangent
):
    frames = queries.shape[1]
    width = residual.shape[2]
    ctx = lax.axis_index("ctx")
    dp = lax.axis_index("dp")
    dp_size = lax.axis_size("dp")
    group = ctx // PER
    member = ctx % PER
    length = lengths[0]

    beside = swap(out_weight, "dp", 1)
    odd = bit_of(dp, 1)
    weight_pair = jnp.concatenate(
        [jnp.where(odd, beside, out_weight), jnp.where(odd, out_weight, beside)], axis=0
    )
    weight_all = lax.all_gather(
        weight_pair,
        "dp",
        axis=0,
        tiled=True,
        axis_index_groups=[list(range(j, dp_size, 2)) for j in range(2)],
    )

    query_scaled = (queries[0].astype(jnp.float32) * (1.0 / math.sqrt(HD))).astype(jnp.bfloat16)
    pieces = []
    for g in range(GROUPS):
        cols = []
        for h in range(GH):
            first = (g * GH + h) * HD
            cols += [attn_keys[0][:, first : first + HD], attn_values[0][:, first : first + HD]]
        cols.append(query_scaled[:, g * GW : (g + 1) * GW])
        pieces.append(jnp.concatenate(cols, axis=1))
    relative = by_group(pieces, group)
    received = [relative[0]] + [swap(relative[k], "ctx", k * PER) for k in range(1, GROUPS)]
    held = jnp.concatenate(by_group(received, group), axis=0)
    own_pairs, query = held[:, : GH * 128], held[:, GH * 128 :]
    rows = own_pairs.shape[0]
    one = (jnp.arange(HD) == 0).astype(jnp.bfloat16)
    query = jnp.concatenate(
        [query.reshape(rows, GH, HD), jnp.broadcast_to(one, (rows, GH, HD))], axis=2
    ).reshape(rows, GH * 128)

    half = rows // 2
    core_own = swap(own_pairs, "ctx", 1)
    from_x = swap(own_pairs, "ctx", 2)
    from_z = swap(own_pairs, "ctx", 4)
    diag_low = swap(from_z[:half], "ctx", 2)
    diag_high = swap(from_x[half:], "ctx", 4)
    near = [own_pairs, from_x, from_z, diag_low, diag_high]
    far = [core_own, swap(jnp.concatenate(near[1:], axis=0), "ctx", 1)]
    order = [0, 2, 4, 6, 1, 3, 5, 7]
    starts = jnp.concatenate(
        [
            jnp.stack([(PER * g + (member ^ k)) * frames for g in range(GROUPS)])
            for k in order
        ]
    )
    positions = (starts[:, None] + jnp.arange(frames, dtype=jnp.int32)[None, :]).reshape(-1, 1)
    masked = (positions >= length) & (jnp.arange(2 * HD) == HD)[None, :]
    bias = jnp.where(masked, MASK_FILL, 0.0).astype(jnp.bfloat16)

    first_half = attention(query, near, bias, 0)
    att_wide, log_total = attention(query, far, bias, 1, first_half)
    att_heads = att_wide.reshape(rows, GH, 2, HD)[:, :, 1].reshape(rows, GW)

    def rows_home(block):
        parts = by_group([block[g * frames : (g + 1) * frames] for g in range(GROUPS)], group)
        back = [parts[0]] + [swap(parts[k], "ctx", k * PER) for k in range(1, GROUPS)]
        return by_group(back, group)

    attended = jnp.concatenate(rows_home(att_heads), axis=1)
    projected = jnp.dot(attended, weight_all, preferred_element_type=jnp.float32)
    residual_mid = (residual[0].astype(jnp.float32) + projected).astype(jnp.bfloat16)
    mid_float = residual_mid.astype(jnp.float32)
    first_frame = ctx * frames
    local_valid = first_frame + jnp.arange(frames, dtype=jnp.int32) < length
    frame_valid = local_valid.astype(jnp.float32)[:, None]
    normed = norm_part(mid_float, norm_gain, frame_valid).astype(jnp.bfloat16)
    side = HALO // 2
    cot = cotangent[0]
    low, high = neighbours(
        jnp.concatenate([normed[:HALO], cot[:side]], axis=0),
        jnp.concatenate([normed[frames - HALO :], cot[frames - side :]], axis=0),
    )
    layer_out, grad_residual, tap_rows = conv_part(
        jnp.clip(length - first_frame, 0, frames).reshape(1),
        normed,
        low,
        high,
        residual_mid,
        cot,
        jnp.concatenate([conv_taps, norm_gain[None]], axis=0),
    )

    grad_att = lax.dot_general(
        grad_residual, weight_all, (((1,), (1,)), ((), ())), preferred_element_type=jnp.float32
    ).astype(jnp.bfloat16)

    parts = by_group([grad_att[:, g * GW : (g + 1) * GW] for g in range(GROUPS)], group)
    moved = [parts[0]] + [swap(parts[k], "ctx", k * PER) for k in range(1, GROUPS)]
    datt = jnp.concatenate(by_group(moved, group), axis=0)
    datt_wide = jnp.pad(
        datt.reshape(rows, GH, HD), ((0, 0), (0, 0), (HD, 0))
    ).reshape(rows, GH * 128)

    tap_count = tap_rows.shape[0]
    mine = jnp.concatenate(
        [
            jnp.concatenate([attended, grad_residual], axis=1),
            jnp.pad(tap_rows, ((0, 0), (0, HW))),
        ],
        axis=0,
    )
    other = swap(mine, "ctx", 1)
    part = lax.dot_general(
        jnp.concatenate([attended, other[:frames, :HW]], axis=0),
        jnp.concatenate([grad_residual, other[:frames, HW:]], axis=0),
        (((0,), (0,)), ((), ())),
        preferred_element_type=jnp.float32,
    )
    part = lax.dynamic_index_in_dim(
        part.reshape(HW // 48, 2, HW // 32, width), ctx % 2, 1, keepdims=False
    ).astype(jnp.bfloat16)
    grad_weight, tap_sum = over_columns(
        part.reshape(HW // 2, width),
        tap_rows.astype(jnp.float32) + other[frames:, :width].astype(jnp.float32),
        ctx,
        dp,
    )
    grad_taps, grad_gain = tap_sum[:KTAPS], tap_sum[KTAPS]

    query_half, far_grad = attention_back(
        query, datt_wide, att_wide, log_total, far, bias, 1, (4 * rows,)
    )
    arrived = swap(far_grad, "ctx", 1)
    query_wide, own, to_x, to_z, far_low, far_high = attention_back(
        query, datt_wide, att_wide, log_total, near, bias, 0,
        (rows, rows, rows, half, half), query_half,
    )
    query_grad = query_wide.reshape(rows, GH, 2, HD)[:, :, 0].reshape(rows, GW)
    far_x = swap(add(far_low, arrived[3 * rows : 3 * rows + half]), "ctx", 2)
    far_z = swap(add(far_high, arrived[3 * rows + half :]), "ctx", 4)
    to_x = to_x.astype(jnp.float32) + arrived[rows : 2 * rows].astype(jnp.float32)
    to_z = to_z.astype(jnp.float32) + arrived[2 * rows : 3 * rows].astype(jnp.float32)
    to_z = jnp.concatenate([to_z[:half] + far_x.astype(jnp.float32), to_z[half:]], axis=0)
    to_x = jnp.concatenate([to_x[:half], to_x[half:] + far_z.astype(jnp.float32)], axis=0)
    pair_sum = (
        own.astype(jnp.float32)
        + arrived[:rows].astype(jnp.float32)
        + swap(to_x.astype(jnp.bfloat16), "ctx", 2).astype(jnp.float32)
        + swap(to_z.astype(jnp.bfloat16), "ctx", 4).astype(jnp.float32)
    ).astype(jnp.bfloat16)
    home = rows_home(jnp.concatenate([pair_sum, query_grad], axis=1))
    keys_out, values_out, queries_out = [], [], []
    for block in home:
        for h in range(GH):
            keys_out.append(block[:, h * 128 : h * 128 + HD])
            values_out.append(block[:, h * 128 + HD : (h + 1) * 128])
        queries_out.append(block[:, GH * 128 :])
    return (
        layer_out[None],
        jnp.concatenate(queries_out, axis=1)[None],
        jnp.concatenate(keys_out, axis=1)[None],
        jnp.concatenate(values_out, axis=1)[None],
        grad_residual[None],
        grad_weight,
        grad_taps,
        grad_gain,
    )


def solution(mesh):
    placed = (
        P("dp", "ctx", None),
        P("dp", "ctx", None),
        P("dp", "ctx", None),
        P("dp", "ctx", None),
        P("dp", None),
        P(),
        P(),
        P("dp"),
        P("dp", "ctx", None),
    )
    return jax.shard_map(
        shards,
        mesh=mesh,
        in_specs=placed,
        out_specs=(
            P("dp", "ctx", None),
            P("dp", "ctx", None),
            P("dp", "ctx", None),
            P("dp", "ctx", None),
            P("dp", "ctx", None),
            P("ctx", "dp"),
            P(),
            P(),
        ),
        check_vma=False,
    )
```

```python
import functools
import math

import jax
import jax.numpy as jnp
from jax import lax
from jax.experimental import pallas as pl
from jax.experimental.pallas import tpu as pltpu
from jax.sharding import PartitionSpec as P

HEADS = 12
HD = 64
KTAPS = 31
HW = 768
GROUPS = 4
GROUP_BITS = 8
MASK_X = 2
MASK_Z = 4
GH = HEADS // GROUPS
GW = GH * HD
HALO = 32
MASK_FILL = -1e30
NORM_EPSILON = 1e-05
VMEM = 48 << 20
NT = (((1,), (1,)), ((), ()))


def swap(block, axis, mask):
    count = lax.axis_size(axis)
    return lax.ppermute(block, axis, [(i, i ^ mask) for i in range(count)])


def bit_of(index, mask):
    return (index & mask) != 0


def by_group(blocks, group):
    first = bit_of(group, 1)
    second = bit_of(group, 2)
    low = [jnp.where(first, blocks[k ^ 1], blocks[k]) for k in range(GROUPS)]
    return [jnp.where(second, low[k ^ 2], low[k]) for k in range(GROUPS)]


def neighbours(first, last):
    count = lax.axis_size("ctx")
    forward = [(i, i + 1) for i in range(count - 1)]
    backward = [(target, source) for source, target in forward]
    return lax.ppermute(last, "ctx", forward), lax.ppermute(first, "ctx", backward)


def norm_part(mid_float, norm_gain, frame_valid):
    row_mean = jnp.mean(mid_float, axis=-1, keepdims=True)
    centred = mid_float - row_mean
    spread = jnp.mean(centred * centred, axis=-1, keepdims=True)
    return centred * lax.rsqrt(spread + NORM_EPSILON) * norm_gain * frame_valid


def conv_kernel(
    valid_ref, normed_ref, low_ref, high_ref, mid_ref, cot_ref, mid_all, cot_all, taps_ref,
    out_ref, grad_ref, rows_ref, frames_buf, conv_buf, mean_buf, scale_buf, back_buf, sum_buf, dot_buf
):
    step = pl.program_id(0)
    frames, width = mid_all.shape
    side = HALO // 2
    f32 = jnp.float32

    @pl.when(step == 0)
    def _():
        mid = mid_all[...].astype(f32)
        mean = jnp.mean(mid, axis=1, keepdims=True)
        centred = mid - mean
        scale = lax.rsqrt(jnp.mean(centred * centred, axis=1, keepdims=True) + NORM_EPSILON)
        mean_buf[...] = jnp.broadcast_to(mean, mean_buf.shape)
        scale_buf[...] = jnp.broadcast_to(scale, scale_buf.shape)
        sum_buf[...] = jnp.zeros_like(sum_buf)
        dot_buf[...] = jnp.zeros_like(dot_buf)

    frames_buf[:HALO] = low_ref[:HALO].astype(f32)
    frames_buf[HALO : HALO + frames] = normed_ref[...].astype(f32)
    frames_buf[HALO + frames :] = high_ref[:HALO].astype(f32)
    conv = jnp.zeros((frames + HALO, 128), f32)
    for k in range(KTAPS):
        conv = conv + taps_ref[k : k + 1, :] * frames_buf[1 + k : 1 + k + frames + HALO, :]
    sig = jax.nn.sigmoid(conv)
    cot = jnp.concatenate([low_ref[HALO:], cot_ref[...], high_ref[HALO:]], axis=0).astype(f32)
    grad_conv = (cot * sig * (1.0 + conv * (1.0 - sig))).astype(jnp.bfloat16).astype(f32)
    conv_buf[...] = grad_conv
    mid = mid_ref[...].astype(f32)
    out_ref[...] = (mid + (conv * sig)[side : side + frames]).astype(jnp.bfloat16)
    own = grad_conv[side : side + frames]
    rows = []
    for k in range(KTAPS):
        window = frames_buf[side + 1 + k : side + 1 + k + frames, :]
        rows.append(jnp.sum(own * window, axis=0, keepdims=True))
    back = jnp.zeros((frames, 128), f32)
    for k in range(KTAPS):
        last = KTAPS - 1 - k
        back = back + taps_ref[last : last + 1, :] * conv_buf[1 + k : 1 + k + frames, :]
    valid = lax.broadcasted_iota(jnp.int32, (frames, 128), 0) < valid_ref[0]
    back = jnp.where(valid, back, 0.0)
    unit = (mid - mean_buf[...]) * scale_buf[...]
    rows.append(jnp.sum(back * unit, axis=0, keepdims=True))
    rows_ref[...] = jnp.concatenate(rows, axis=0).astype(jnp.bfloat16)
    back = back * taps_ref[KTAPS : KTAPS + 1, :]
    back_buf[step] = back
    sum_buf[...] += back
    dot_buf[...] += back * unit

    @pl.when(step == pl.num_programs(0) - 1)
    def _():
        shift = jnp.mean(sum_buf[...], axis=1, keepdims=True) * (128.0 / width)
        slope = jnp.mean(dot_buf[...], axis=1, keepdims=True) * (128.0 / width)
        for c in range(width // 128):
            at = slice(c * 128, (c + 1) * 128)
            unit = (mid_all[:, at].astype(f32) - mean_buf[...]) * scale_buf[...]
            grad = scale_buf[...] * (back_buf[c] - shift - unit * slope)
            grad_ref[:, at] = (cot_all[:, at].astype(f32) + grad).astype(jnp.bfloat16)


def conv_part(valid_count, normed, low, high, mid, cot, taps):
    frames, width = mid.shape
    block = pl.BlockSpec((frames, 128), lambda c: (0, c))
    edge = pl.BlockSpec((low.shape[0], 128), lambda c: (0, c))
    whole = pl.BlockSpec((frames, width), lambda c: (0, 0))
    tap = pl.BlockSpec((KTAPS + 1, 128), lambda c: (0, c))
    square = pltpu.VMEM((frames, 128), jnp.float32)
    return pl.pallas_call(
        conv_kernel,
        grid=(width // 128,),
        in_specs=[
            pl.BlockSpec(memory_space=pltpu.SMEM), block, edge, edge, block, block, whole, whole, tap,
        ],
        out_specs=[block, whole, tap],
        out_shape=[
            jax.ShapeDtypeStruct((frames, width), jnp.bfloat16),
            jax.ShapeDtypeStruct((frames, width), jnp.bfloat16),
            jax.ShapeDtypeStruct((KTAPS + 1, width), jnp.bfloat16),
        ],
        scratch_shapes=[
            pltpu.VMEM((frames + 2 * HALO, 128), jnp.float32),
            pltpu.VMEM((frames + HALO, 128), jnp.float32),
            square,
            square,
            pltpu.VMEM((width // 128, frames, 128), jnp.float32),
            square,
            square,
        ],
        cost_estimate=pl.CostEstimate(
            flops=200 * frames * width, bytes_accessed=1 << 22, transcendentals=frames * width
        ),
        compiler_params=pltpu.CompilerParams(vmem_limit_bytes=VMEM),
    )(valid_count, normed, low, high, mid, cot, mid, cot, taps)


def lanes_of(shape):
    return lax.broadcasted_iota(jnp.int32, shape, 1)


def rows_of(refs):
    return refs[0][...] if len(refs) == 1 else jnp.concatenate([ref[...] for ref in refs], axis=0)


def head_of(block, h, pad, below=False):
    cols = block[:, h * HD : (h + 1) * HD]
    fill = jnp.broadcast_to(pad, cols.shape).astype(block.dtype)
    return jnp.concatenate([fill, cols] if below else [cols, fill], axis=1)


def unit_lane():
    return jnp.where(lanes_of((1, HD)) == 0, 1.0, 0.0)


def forward_kernel(count, merge, *refs):
    q_ref, kv_refs, bias_ref = refs[0], refs[1 : 1 + count], refs[1 + count]
    kv_all = rows_of(kv_refs)
    bias = bias_ref[...]
    lane = lanes_of(bias.shape)
    q_all = q_ref[...]
    atts, logs = [], []
    for h in range(GH):
        at = slice(h * 128, (h + 1) * 128)
        kv = kv_all[:, at]
        k_aug = jnp.where(lane < HD, kv, bias)
        v_aug = jnp.where(lane < HD, jnp.ones_like(kv), kv)
        q = head_of(q_all, h, unit_lane())
        scores = lax.dot_general(q, k_aug, NT, preferred_element_type=jnp.float32)
        row_max = jnp.max(scores, axis=1, keepdims=True)
        weights = jnp.exp(scores - row_max).astype(jnp.bfloat16)
        acc = jnp.dot(weights, v_aug, preferred_element_type=jnp.float32)
        total = pltpu.roll(acc, HD, 1)
        low = lanes_of(acc.shape) < HD
        out = jnp.where(low, row_max + jnp.log(acc), acc / total)
        if not merge:
            refs[-1][:, at] = out
            continue
        prev = refs[2 + count][:, at]
        mine = jnp.where(low, out, pltpu.roll(out, HD, 1))
        theirs = jnp.where(low, prev, pltpu.roll(prev, HD, 1))
        top = jnp.maximum(mine, theirs)
        both = top + jnp.log(jnp.exp(mine - top) + jnp.exp(theirs - top))
        merged = out * jnp.exp(mine - both) + prev * jnp.exp(theirs - both)
        atts.append(merged[:, HD:])
        logs.append(jnp.transpose(both)[:1])
    if merge:
        att_ref, log_ref = refs[3 + count :]
        att_ref[...] = jnp.concatenate(atts, axis=1).astype(jnp.bfloat16)
        log_ref[...] = jnp.concatenate(logs + logs[:1] * (8 - GH), axis=0)


def attention(query, pieces, bias, half, prev=None, block=256):
    n, keys = query.shape[0], bias.shape[0] // 2
    row = pl.BlockSpec((block, GW), lambda i: (i, 0))
    wide = pl.BlockSpec((block, GH * 128), lambda i: (i, 0))
    ins = [row]
    ins += [pl.BlockSpec(piece.shape, lambda i: (0, 0)) for piece in pieces]
    ins.append(pl.BlockSpec((keys, 128), lambda i: (half, 0)))
    args = [query, *pieces, bias]
    out_specs, out_shape = wide, jax.ShapeDtypeStruct((n, GH * 128), jnp.float32)
    if prev is not None:
        ins.append(wide)
        args.append(prev)
        out_specs = [row, pl.BlockSpec((8, block), lambda i: (0, i))]
        out_shape = [
            jax.ShapeDtypeStruct((n, GW), jnp.bfloat16),
            jax.ShapeDtypeStruct((8, n), jnp.float32),
        ]
    return pl.pallas_call(
        functools.partial(forward_kernel, len(pieces), prev is not None),
        grid=(n // block,),
        in_specs=ins,
        out_specs=out_specs,
        out_shape=out_shape,
        cost_estimate=pl.CostEstimate(
            flops=8 * n * keys * GH * 128, bytes_accessed=1 << 22, transcendentals=n * keys * GH
        ),
        compiler_params=pltpu.CompilerParams(vmem_limit_bytes=VMEM),
    )(*args)


def backward_kernel(count, last, *refs):
    q_ref, do_ref, att_ref, log_ref = refs[:4]
    kv_refs, bias_ref = refs[4 : 4 + count], refs[4 + count]
    outs = refs[5 + count :]
    products = do_ref[...].astype(jnp.float32) * att_ref[...].astype(jnp.float32)
    products = jnp.transpose(products)
    q_all, do_all = q_ref[...], do_ref[...]
    kv_all = rows_of(kv_refs)
    bias_all = bias_ref[...]
    step = kv_all.shape[0] // 2
    dq_rows = []
    for h in range(GH):
        at = slice(h * 128, (h + 1) * 128)
        q = head_of(q_all, h, unit_lane())
        q_only = head_of(q_all, h, 0.0)
        do = head_of(do_all, h, 0.0, below=True)
        log_row = log_ref[h : h + 1, :]
        delta = jnp.sum(products[h * HD : (h + 1) * HD], axis=0, keepdims=True)
        grads, dq = [], None
        for part in range(2):
            kv = kv_all[part * step : (part + 1) * step, at]
            bias = bias_all[part * step : (part + 1) * step]
            k_aug = jnp.where(lanes_of(kv.shape) < HD, kv, bias)
            scores = lax.dot_general(k_aug, q, NT, preferred_element_type=jnp.float32)
            prob = jnp.exp(scores - log_row)
            grad_prob = lax.dot_general(kv, do, NT, preferred_element_type=jnp.float32)
            grad_score = (prob * (grad_prob - delta)).astype(jnp.bfloat16)
            grads.append(
                (
                    jnp.dot(grad_score, q_only, preferred_element_type=jnp.float32)
                    + jnp.dot(prob.astype(jnp.bfloat16), do, preferred_element_type=jnp.float32)
                ).astype(jnp.bfloat16)
            )
            term = jnp.dot(jnp.transpose(kv)[:HD], grad_score, preferred_element_type=jnp.float32)
            dq = term if dq is None else dq + term
        dq_rows.append(dq)
        start = 0
        flat = jnp.concatenate(grads, axis=0)
        for ref in outs[1 + last :]:
            ref[:, at] = flat[start : start + ref.shape[0]]
            start += ref.shape[0]
    dq = jnp.concatenate(dq_rows, axis=0)
    if last:
        outs[1][...] = (jnp.transpose(dq + outs[0][...]) * (1.0 / math.sqrt(HD))).astype(
            jnp.bfloat16
        )
    else:
        outs[0][...] = dq


def attention_back(query, datt, att, log, pieces, bias, half, splits, prev=None):
    n, keys = query.shape[0], bias.shape[0] // 2

    def whole(shape):
        return pl.BlockSpec(shape, lambda i: (0,) * len(shape))

    args = [query, datt, att, log, *pieces]
    ins = [whole(arg.shape) for arg in args]
    args.append(bias)
    ins.append(pl.BlockSpec((keys, 128), lambda i: (half, 0)))
    if prev is None:
        shapes = [jax.ShapeDtypeStruct((GW, n), jnp.float32)]
    else:
        args.append(prev)
        ins.append(whole(prev.shape))
        shapes = [jax.ShapeDtypeStruct((n, GW), jnp.bfloat16)]
    shapes += [jax.ShapeDtypeStruct((size, GH * 128), jnp.bfloat16) for size in splits]
    return pl.pallas_call(
        functools.partial(backward_kernel, len(pieces), prev is not None),
        grid=(1,),
        in_specs=ins,
        out_specs=[whole(shape.shape) for shape in shapes],
        out_shape=shapes,
        cost_estimate=pl.CostEstimate(
            flops=20 * n * keys * GH * 128, bytes_accessed=1 << 22, transcendentals=n * keys * GH
        ),
        compiler_params=pltpu.CompilerParams(vmem_limit_bytes=VMEM),
    )(*args)


def add(first, second):
    return (first.astype(jnp.float32) + second.astype(jnp.float32)).astype(first.dtype)


def pick(block, dim, mask, index):
    mine = (index & mask) // mask
    kept = lax.dynamic_index_in_dim(block, mine, dim, keepdims=False)
    sent = lax.dynamic_index_in_dim(block, 1 - mine, dim, keepdims=False)
    return kept, sent


def along_y(part, rows, along):
    quarter = rows.shape[1] // 4
    joined = jnp.concatenate([part, rows.astype(jnp.bfloat16)], axis=0)
    blocks = by_group([joined[:, j * quarter : (j + 1) * quarter] for j in range(4)], along)
    return [blocks[0]] + [swap(blocks[k], "dp", 2 * k) for k in range(1, 4)]


def first_half_step(quarters, count, ctx):
    total = quarters[0].astype(jnp.float32)
    for block in quarters[1:]:
        total = total + block.astype(jnp.float32)
    rows = total[-count:].astype(jnp.bfloat16)
    part = total[:-count].astype(jnp.bfloat16).reshape(2, 2, 2, 2, -1, total.shape[1])
    kept, sent = pick(part, 3, 2, ctx)
    joined = jnp.concatenate([sent.reshape(-1, total.shape[1]), rows], axis=0)
    return swap(joined, "ctx", 2), kept, rows


def over_columns(part, other, rows, ctx, dp):
    count, quarter = rows.shape
    for dim, mask in ((2, 4), (1, 8), (0, 16), (0, 0)):
        part = add(part, other[:-count].reshape(part.shape))
        rows = rows.astype(jnp.float32) + other[-count:].astype(jnp.float32)
        if mask:
            part, sent = pick(part, dim, mask, ctx)
            rows = rows.astype(jnp.bfloat16)
            other = swap(jnp.concatenate([sent.reshape(-1, quarter), rows], axis=0), "ctx", mask)
    joined = jnp.concatenate([part, rows.astype(jnp.bfloat16)], axis=0)
    total = joined.astype(jnp.float32) + swap(joined, "dp", 1).astype(jnp.float32)
    half = quarter // 2
    weight = jnp.where(bit_of(dp, 1), total[:-count, half:], total[:-count, :half])
    rows = total[-count:]
    spread = [rows] + [swap(rows, "dp", 2 * k) for k in range(1, 4)]
    return weight, jnp.concatenate(by_group(spread, dp // 2), axis=1)


def shards(
    queries, attn_keys, attn_values, residual, out_weight, conv_taps, norm_gain, lengths, cotangent
):
    frames = queries.shape[1]
    width = residual.shape[2]
    ctx = lax.axis_index("ctx")
    dp = lax.axis_index("dp")
    dp_size = lax.axis_size("dp")
    group = (ctx // GROUP_BITS) % GROUPS
    length = lengths[0]

    query_scaled = (queries[0].astype(jnp.float32) * (1.0 / math.sqrt(HD))).astype(jnp.bfloat16)
    pieces = []
    for g in range(GROUPS):
        cols = []
        for h in range(GH):
            first = (g * GH + h) * HD
            cols += [attn_keys[0][:, first : first + HD], attn_values[0][:, first : first + HD]]
        cols.append(query_scaled[:, g * GW : (g + 1) * GW])
        pieces.append(jnp.concatenate(cols, axis=1))
    relative = by_group(pieces, group)
    received = [relative[0]] + [swap(relative[k], "ctx", k * GROUP_BITS) for k in range(1, GROUPS)]
    held = jnp.concatenate(by_group(received, group), axis=0)
    own_pairs, query = held[:, : GH * 128], held[:, GH * 128 :]
    rows = own_pairs.shape[0]
    beside = swap(out_weight, "dp", 1)
    odd = bit_of(dp, 1)
    weight_pair = jnp.concatenate(
        [jnp.where(odd, beside, out_weight), jnp.where(odd, out_weight, beside)], axis=0
    )
    own_pairs, weight_pair = lax.optimization_barrier((own_pairs, weight_pair))
    half = rows // 2
    core_own = swap(own_pairs, "ctx", 1)
    from_x = swap(own_pairs, "ctx", MASK_X)
    from_z = swap(own_pairs, "ctx", MASK_Z)
    weight_near = swap(weight_pair, "dp", 2)
    weight_far = swap(weight_pair, "dp", 6)
    from_x, from_z, weight_near, weight_far = lax.optimization_barrier(
        (from_x, from_z, weight_near, weight_far)
    )
    order = [0, MASK_X, MASK_Z, MASK_X ^ MASK_Z]
    outside = ctx & ~((GROUPS - 1) * GROUP_BITS)
    starts = jnp.concatenate(
        [
            jnp.stack([((outside ^ k) + g * GROUP_BITS) * frames for g in range(GROUPS)])
            for k in order + [k ^ 1 for k in order]
        ]
    )
    positions = (starts[:, None] + jnp.arange(frames, dtype=jnp.int32)[None, :]).reshape(-1, 1)
    masked = (positions >= length) & (jnp.arange(2 * HD) == HD)[None, :]
    bias = jnp.where(masked, MASK_FILL, 0.0).astype(jnp.bfloat16)
    diag_low = swap(from_z[:half], "ctx", MASK_X)
    diag_high = swap(from_x[half:], "ctx", MASK_Z)
    middle = weight_pair.shape[0] // 2
    weight_low = swap(weight_near[:middle], "dp", 6)
    weight_high = swap(weight_far[middle:], "dp", 2)
    diag_low, diag_high, weight_low, weight_high, query = lax.optimization_barrier(
        (diag_low, diag_high, weight_low, weight_high, query)
    )
    near = [own_pairs, from_x, from_z, diag_low, diag_high]
    far = [core_own, swap(jnp.concatenate(near[1:], axis=0), "ctx", 1)]

    first_half = attention(query, near, bias, 0)
    att_heads, log_total = attention(query, far, bias, 1, first_half)

    def rows_home(block):
        parts = by_group([block[g * frames : (g + 1) * frames] for g in range(GROUPS)], group)
        back = [parts[0]] + [swap(parts[k], "ctx", k * GROUP_BITS) for k in range(1, GROUPS)]
        return by_group(back, group)

    attended = jnp.concatenate(rows_home(att_heads), axis=1)
    weight_across = jnp.concatenate([weight_low, weight_high], axis=0)
    weight_parts = [weight_pair, weight_near, weight_across, weight_far]
    weight_all = jnp.concatenate(by_group(weight_parts, dp // 2), axis=0)
    projected = jnp.dot(attended, weight_all, preferred_element_type=jnp.float32)
    residual_mid = (residual[0].astype(jnp.float32) + projected).astype(jnp.bfloat16)
    mid_float = residual_mid.astype(jnp.float32)
    first_frame = ctx * frames
    local_valid = first_frame + jnp.arange(frames, dtype=jnp.int32) < length
    frame_valid = local_valid.astype(jnp.float32)[:, None]
    normed = norm_part(mid_float, norm_gain, frame_valid).astype(jnp.bfloat16)
    side = HALO // 2
    cot = cotangent[0]
    low, high = neighbours(
        jnp.concatenate([normed[:HALO], cot[:side]], axis=0),
        jnp.concatenate([normed[frames - HALO :], cot[frames - side :]], axis=0),
    )
    layer_out, grad_residual, tap_rows = conv_part(
        jnp.clip(length - first_frame, 0, frames).reshape(1),
        normed,
        low,
        high,
        residual_mid,
        cot,
        jnp.concatenate([conv_taps, norm_gain[None]], axis=0),
    )

    grad_att = lax.dot_general(
        grad_residual, weight_all, (((1,), (1,)), ((), ())), preferred_element_type=jnp.float32
    ).astype(jnp.bfloat16)

    parts = by_group([grad_att[:, g * GW : (g + 1) * GW] for g in range(GROUPS)], group)
    moved = [parts[0]] + [swap(parts[k], "ctx", k * GROUP_BITS) for k in range(1, GROUPS)]
    datt = jnp.concatenate(by_group(moved, group), axis=0)

    att_other = swap(attended, "ctx", 1)
    grad_mine, tap_mine, unused = lax.optimization_barrier((grad_residual, tap_rows, grad_att))
    grad_other = swap(grad_mine, "ctx", 1)
    tap_other = swap(tap_mine, "ctx", 1)
    contract = (((0,), (0,)), ((), ()))
    part = lax.dot_general(
        attended, grad_residual, contract, preferred_element_type=jnp.float32
    ) + lax.dot_general(att_other, grad_other, contract, preferred_element_type=jnp.float32)
    part = lax.dynamic_index_in_dim(
        part.reshape(HW // 48, 2, HW // 32, width), ctx % 2, 1, keepdims=False
    ).astype(jnp.bfloat16)
    along = dp // 2
    taps = tap_mine.astype(jnp.float32) + tap_other.astype(jnp.float32)
    quarters = along_y(part.reshape(HW // 2, width), taps, along)

    query_half, far_grad = attention_back(
        query, datt, att_heads, log_total, far, bias, 1, (4 * rows,)
    )
    arrived = swap(far_grad, "ctx", 1)
    query_grad, own, to_x, to_z, far_low, far_high = attention_back(
        query, datt, att_heads, log_total, near, bias, 0,
        (rows, rows, rows, half, half), query_half,
    )
    quarters, unused = lax.optimization_barrier((quarters, own))
    sent, kept, taps = first_half_step(quarters, taps.shape[0], ctx)
    sent, unused = lax.optimization_barrier((sent, arrived))
    grad_weight, tap_sum = over_columns(kept, sent, taps, ctx, dp)
    grad_taps, grad_gain = tap_sum[:KTAPS], tap_sum[KTAPS]

    far_x = swap(add(far_low, arrived[3 * rows : 3 * rows + half]), "ctx", MASK_X)
    far_z = swap(add(far_high, arrived[3 * rows + half :]), "ctx", MASK_Z)
    to_x = to_x.astype(jnp.float32) + arrived[rows : 2 * rows].astype(jnp.float32)
    to_z = to_z.astype(jnp.float32) + arrived[2 * rows : 3 * rows].astype(jnp.float32)
    to_z = jnp.concatenate([to_z[:half] + far_x.astype(jnp.float32), to_z[half:]], axis=0)
    to_x = jnp.concatenate([to_x[:half], to_x[half:] + far_z.astype(jnp.float32)], axis=0)
    pair_sum = (
        own.astype(jnp.float32)
        + arrived[:rows].astype(jnp.float32)
        + swap(to_x.astype(jnp.bfloat16), "ctx", MASK_X).astype(jnp.float32)
        + swap(to_z.astype(jnp.bfloat16), "ctx", MASK_Z).astype(jnp.float32)
    ).astype(jnp.bfloat16)
    home = rows_home(jnp.concatenate([pair_sum, query_grad], axis=1))
    keys_out, values_out, queries_out = [], [], []
    for block in home:
        for h in range(GH):
            keys_out.append(block[:, h * 128 : h * 128 + HD])
            values_out.append(block[:, h * 128 + HD : (h + 1) * 128])
        queries_out.append(block[:, GH * 128 :])
    return (
        layer_out[None],
        jnp.concatenate(queries_out, axis=1)[None],
        jnp.concatenate(keys_out, axis=1)[None],
        jnp.concatenate(values_out, axis=1)[None],
        grad_residual[None],
        grad_weight,
        grad_taps,
        grad_gain,
    )


def solution(mesh):
    placed = (
        P("dp", "ctx", None),
        P("dp", "ctx", None),
        P("dp", "ctx", None),
        P("dp", "ctx", None),
        P("dp", None),
        P(),
        P(),
        P("dp"),
        P("dp", "ctx", None),
    )
    return jax.shard_map(
        shards,
        mesh=mesh,
        in_specs=placed,
        out_specs=(
            P("dp", "ctx", None),
            P("dp", "ctx", None),
            P("dp", "ctx", None),
            P("dp", "ctx", None),
            P("dp", "ctx", None),
            P("ctx", "dp"),
            P(),
            P(),
        ),
        check_vma=False,
    )
```

```python
import functools
import math

import jax
import jax.numpy as jnp
from jax import lax
from jax.experimental import pallas as pl
from jax.experimental.pallas import tpu as pltpu
from jax.sharding import PartitionSpec as P

HEADS = 12
HD = 64
KTAPS = 31
HW = 768
GROUPS = 4
GROUP_BITS = 8
MASK_X = 2
MASK_Z = 4
GH = HEADS // GROUPS
GW = GH * HD
HALO = 32
MASK_FILL = -1e30
NORM_EPSILON = 1e-05
VMEM = 48 << 20
NT = (((1,), (1,)), ((), ()))


def swap(block, axis, mask):
    count = lax.axis_size(axis)
    return lax.ppermute(block, axis, [(i, i ^ mask) for i in range(count)])


def bit_of(index, mask):
    return (index & mask) != 0


def by_group(blocks, group):
    first = bit_of(group, 1)
    second = bit_of(group, 2)
    low = [jnp.where(first, blocks[k ^ 1], blocks[k]) for k in range(GROUPS)]
    return [jnp.where(second, low[k ^ 2], low[k]) for k in range(GROUPS)]


def neighbours(first, last):
    count = lax.axis_size("ctx")
    forward = [(i, i + 1) for i in range(count - 1)]
    backward = [(target, source) for source, target in forward]
    return lax.ppermute(last, "ctx", forward), lax.ppermute(first, "ctx", backward)


def exchange(parts):
    size = parts[0].shape[0]
    near = swap(jnp.concatenate([parts[1], parts[2][: size // 2]], axis=0), "ctx", GROUP_BITS)
    far = swap(jnp.concatenate([parts[3], parts[2][size // 2 :]], axis=0), "ctx", 3 * GROUP_BITS)
    low = swap(near[size:], "ctx", 3 * GROUP_BITS)
    high = swap(far[size:], "ctx", GROUP_BITS)
    return [parts[0], near[:size], jnp.concatenate([low, high], axis=0), far[:size]]


def norm_part(mid_float, norm_gain, frame_valid):
    row_mean = jnp.mean(mid_float, axis=-1, keepdims=True)
    centred = mid_float - row_mean
    spread = jnp.mean(centred * centred, axis=-1, keepdims=True)
    return centred * lax.rsqrt(spread + NORM_EPSILON) * norm_gain * frame_valid


def conv_kernel(
    valid_ref, normed_ref, low_ref, high_ref, mid_ref, cot_ref, mid_all, cot_all, taps_ref,
    out_ref, grad_ref, rows_ref, frames_buf, conv_buf, mean_buf, scale_buf, back_buf, sum_buf, dot_buf
):
    step = pl.program_id(0)
    frames, width = mid_all.shape
    side = HALO // 2
    f32 = jnp.float32

    @pl.when(step == 0)
    def _():
        mid = mid_all[...].astype(f32)
        mean = jnp.mean(mid, axis=1, keepdims=True)
        centred = mid - mean
        scale = lax.rsqrt(jnp.mean(centred * centred, axis=1, keepdims=True) + NORM_EPSILON)
        mean_buf[...] = jnp.broadcast_to(mean, mean_buf.shape)
        scale_buf[...] = jnp.broadcast_to(scale, scale_buf.shape)
        sum_buf[...] = jnp.zeros_like(sum_buf)
        dot_buf[...] = jnp.zeros_like(dot_buf)

    frames_buf[:HALO] = low_ref[:HALO].astype(f32)
    frames_buf[HALO : HALO + frames] = normed_ref[...].astype(f32)
    frames_buf[HALO + frames :] = high_ref[:HALO].astype(f32)
    conv = jnp.zeros((frames + HALO, 128), f32)
    for k in range(KTAPS):
        conv = conv + taps_ref[k : k + 1, :] * frames_buf[1 + k : 1 + k + frames + HALO, :]
    sig = jax.nn.sigmoid(conv)
    cot = jnp.concatenate([low_ref[HALO:], cot_ref[...], high_ref[HALO:]], axis=0).astype(f32)
    grad_conv = (cot * sig * (1.0 + conv * (1.0 - sig))).astype(jnp.bfloat16).astype(f32)
    conv_buf[...] = grad_conv
    mid = mid_ref[...].astype(f32)
    out_ref[...] = (mid + (conv * sig)[side : side + frames]).astype(jnp.bfloat16)
    own = grad_conv[side : side + frames]
    rows = []
    for k in range(KTAPS):
        window = frames_buf[side + 1 + k : side + 1 + k + frames, :]
        rows.append(jnp.sum(own * window, axis=0, keepdims=True))
    back = jnp.zeros((frames, 128), f32)
    for k in range(KTAPS):
        last = KTAPS - 1 - k
        back = back + taps_ref[last : last + 1, :] * conv_buf[1 + k : 1 + k + frames, :]
    valid = lax.broadcasted_iota(jnp.int32, (frames, 128), 0) < valid_ref[0]
    back = jnp.where(valid, back, 0.0)
    unit = (mid - mean_buf[...]) * scale_buf[...]
    rows.append(jnp.sum(back * unit, axis=0, keepdims=True))
    rows_ref[...] = jnp.concatenate(rows, axis=0).astype(jnp.bfloat16)
    back = back * taps_ref[KTAPS : KTAPS + 1, :]
    back_buf[step] = back
    sum_buf[...] += back
    dot_buf[...] += back * unit

    @pl.when(step == pl.num_programs(0) - 1)
    def _():
        shift = jnp.mean(sum_buf[...], axis=1, keepdims=True) * (128.0 / width)
        slope = jnp.mean(dot_buf[...], axis=1, keepdims=True) * (128.0 / width)
        for c in range(width // 128):
            at = slice(c * 128, (c + 1) * 128)
            unit = (mid_all[:, at].astype(f32) - mean_buf[...]) * scale_buf[...]
            grad = scale_buf[...] * (back_buf[c] - shift - unit * slope)
            grad_ref[:, at] = (cot_all[:, at].astype(f32) + grad).astype(jnp.bfloat16)


def conv_part(valid_count, normed, low, high, mid, cot, taps):
    frames, width = mid.shape
    block = pl.BlockSpec((frames, 128), lambda c: (0, c))
    edge = pl.BlockSpec((low.shape[0], 128), lambda c: (0, c))
    whole = pl.BlockSpec((frames, width), lambda c: (0, 0))
    tap = pl.BlockSpec((KTAPS + 1, 128), lambda c: (0, c))
    square = pltpu.VMEM((frames, 128), jnp.float32)
    return pl.pallas_call(
        conv_kernel,
        grid=(width // 128,),
        in_specs=[
            pl.BlockSpec(memory_space=pltpu.SMEM), block, edge, edge, block, block, whole, whole, tap,
        ],
        out_specs=[block, whole, tap],
        out_shape=[
            jax.ShapeDtypeStruct((frames, width), jnp.bfloat16),
            jax.ShapeDtypeStruct((frames, width), jnp.bfloat16),
            jax.ShapeDtypeStruct((KTAPS + 1, width), jnp.bfloat16),
        ],
        scratch_shapes=[
            pltpu.VMEM((frames + 2 * HALO, 128), jnp.float32),
            pltpu.VMEM((frames + HALO, 128), jnp.float32),
            square,
            square,
            pltpu.VMEM((width // 128, frames, 128), jnp.float32),
            square,
            square,
        ],
        cost_estimate=pl.CostEstimate(
            flops=200 * frames * width, bytes_accessed=1 << 22, transcendentals=frames * width
        ),
        compiler_params=pltpu.CompilerParams(vmem_limit_bytes=VMEM),
    )(valid_count, normed, low, high, mid, cot, mid, cot, taps)


def lanes_of(shape):
    return lax.broadcasted_iota(jnp.int32, shape, 1)


def rows_of(refs):
    return refs[0][...] if len(refs) == 1 else jnp.concatenate([ref[...] for ref in refs], axis=0)


def head_of(block, h, pad, below=False):
    cols = block[:, h * HD : (h + 1) * HD]
    fill = jnp.broadcast_to(pad, cols.shape).astype(block.dtype)
    return jnp.concatenate([fill, cols] if below else [cols, fill], axis=1)


def unit_lane():
    return jnp.where(lanes_of((1, HD)) == 0, 1.0, 0.0)


def forward_kernel(count, merge, *refs):
    q_ref, kv_refs, bias_ref = refs[0], refs[1 : 1 + count], refs[1 + count]
    kv_all = rows_of(kv_refs)
    bias = bias_ref[...]
    lane = lanes_of(bias.shape)
    q_all = q_ref[...]
    atts, logs = [], []
    for h in range(GH):
        at = slice(h * 128, (h + 1) * 128)
        kv = kv_all[:, at]
        k_aug = jnp.where(lane < HD, kv, bias)
        v_aug = jnp.where(lane < HD, jnp.ones_like(kv), kv)
        q = head_of(q_all, h, unit_lane())
        scores = lax.dot_general(q, k_aug, NT, preferred_element_type=jnp.float32)
        row_max = jnp.max(scores, axis=1, keepdims=True)
        weights = jnp.exp(scores - row_max).astype(jnp.bfloat16)
        acc = jnp.dot(weights, v_aug, preferred_element_type=jnp.float32)
        total = pltpu.roll(acc, HD, 1)
        low = lanes_of(acc.shape) < HD
        out = jnp.where(low, row_max + jnp.log(acc), acc / total)
        if not merge:
            refs[-1][:, at] = out
            continue
        prev = refs[2 + count][:, at]
        mine = jnp.where(low, out, pltpu.roll(out, HD, 1))
        theirs = jnp.where(low, prev, pltpu.roll(prev, HD, 1))
        top = jnp.maximum(mine, theirs)
        both = top + jnp.log(jnp.exp(mine - top) + jnp.exp(theirs - top))
        merged = out * jnp.exp(mine - both) + prev * jnp.exp(theirs - both)
        atts.append(merged[:, HD:])
        logs.append(jnp.transpose(both)[:1])
    if merge:
        att_ref, log_ref = refs[3 + count :]
        att_ref[...] = jnp.concatenate(atts, axis=1).astype(jnp.bfloat16)
        log_ref[...] = jnp.concatenate(logs + logs[:1] * (8 - GH), axis=0)


def attention(query, pieces, bias, half, prev=None, block=256):
    n, keys = query.shape[0], bias.shape[0] // 2
    row = pl.BlockSpec((block, GW), lambda i: (i, 0))
    wide = pl.BlockSpec((block, GH * 128), lambda i: (i, 0))
    ins = [row]
    ins += [pl.BlockSpec(piece.shape, lambda i: (0, 0)) for piece in pieces]
    ins.append(pl.BlockSpec((keys, 128), lambda i: (half, 0)))
    args = [query, *pieces, bias]
    out_specs, out_shape = wide, jax.ShapeDtypeStruct((n, GH * 128), jnp.float32)
    if prev is not None:
        ins.append(wide)
        args.append(prev)
        out_specs = [row, pl.BlockSpec((8, block), lambda i: (0, i))]
        out_shape = [
            jax.ShapeDtypeStruct((n, GW), jnp.bfloat16),
            jax.ShapeDtypeStruct((8, n), jnp.float32),
        ]
    return pl.pallas_call(
        functools.partial(forward_kernel, len(pieces), prev is not None),
        grid=(n // block,),
        in_specs=ins,
        out_specs=out_specs,
        out_shape=out_shape,
        cost_estimate=pl.CostEstimate(
            flops=8 * n * keys * GH * 128, bytes_accessed=1 << 22, transcendentals=n * keys * GH
        ),
        compiler_params=pltpu.CompilerParams(vmem_limit_bytes=VMEM),
    )(*args)


def backward_kernel(count, last, *refs):
    q_ref, do_ref, att_ref, log_ref = refs[:4]
    kv_refs, bias_ref = refs[4 : 4 + count], refs[4 + count]
    outs = refs[5 + count :]
    products = do_ref[...].astype(jnp.float32) * att_ref[...].astype(jnp.float32)
    products = jnp.transpose(products)
    q_all, do_all = q_ref[...], do_ref[...]
    kv_all = rows_of(kv_refs)
    bias_all = bias_ref[...]
    step = kv_all.shape[0] // 2
    dq_rows = []
    for h in range(GH):
        at = slice(h * 128, (h + 1) * 128)
        q = head_of(q_all, h, unit_lane())
        q_only = head_of(q_all, h, 0.0)
        do = head_of(do_all, h, 0.0, below=True)
        log_row = log_ref[h : h + 1, :]
        delta = jnp.sum(products[h * HD : (h + 1) * HD], axis=0, keepdims=True)
        grads, dq = [], None
        for part in range(2):
            kv = kv_all[part * step : (part + 1) * step, at]
            bias = bias_all[part * step : (part + 1) * step]
            k_aug = jnp.where(lanes_of(kv.shape) < HD, kv, bias)
            scores = lax.dot_general(k_aug, q, NT, preferred_element_type=jnp.float32)
            prob = jnp.exp(scores - log_row)
            grad_prob = lax.dot_general(kv, do, NT, preferred_element_type=jnp.float32)
            grad_score = (prob * (grad_prob - delta)).astype(jnp.bfloat16)
            grads.append(
                (
                    jnp.dot(grad_score, q_only, preferred_element_type=jnp.float32)
                    + jnp.dot(prob.astype(jnp.bfloat16), do, preferred_element_type=jnp.float32)
                ).astype(jnp.bfloat16)
            )
            term = jnp.dot(jnp.transpose(kv)[:HD], grad_score, preferred_element_type=jnp.float32)
            dq = term if dq is None else dq + term
        dq_rows.append(dq)
        start = 0
        flat = jnp.concatenate(grads, axis=0)
        for ref in outs[1 + last :]:
            ref[:, at] = flat[start : start + ref.shape[0]]
            start += ref.shape[0]
    dq = jnp.concatenate(dq_rows, axis=0)
    if last:
        outs[1][...] = (jnp.transpose(dq + outs[0][...]) * (1.0 / math.sqrt(HD))).astype(
            jnp.bfloat16
        )
    else:
        outs[0][...] = dq


def attention_back(query, datt, att, log, pieces, bias, half, splits, prev=None):
    n, keys = query.shape[0], bias.shape[0] // 2

    def whole(shape):
        return pl.BlockSpec(shape, lambda i: (0,) * len(shape))

    args = [query, datt, att, log, *pieces]
    ins = [whole(arg.shape) for arg in args]
    args.append(bias)
    ins.append(pl.BlockSpec((keys, 128), lambda i: (half, 0)))
    if prev is None:
        shapes = [jax.ShapeDtypeStruct((GW, n), jnp.float32)]
    else:
        args.append(prev)
        ins.append(whole(prev.shape))
        shapes = [jax.ShapeDtypeStruct((n, GW), jnp.bfloat16)]
    shapes += [jax.ShapeDtypeStruct((size, GH * 128), jnp.bfloat16) for size in splits]
    return pl.pallas_call(
        functools.partial(backward_kernel, len(pieces), prev is not None),
        grid=(1,),
        in_specs=ins,
        out_specs=[whole(shape.shape) for shape in shapes],
        out_shape=shapes,
        cost_estimate=pl.CostEstimate(
            flops=20 * n * keys * GH * 128, bytes_accessed=1 << 22, transcendentals=n * keys * GH
        ),
        compiler_params=pltpu.CompilerParams(vmem_limit_bytes=VMEM),
    )(*args)


def add(first, second):
    return (first.astype(jnp.float32) + second.astype(jnp.float32)).astype(first.dtype)


def pick(block, dim, mask, index):
    mine = (index & mask) // mask
    kept = lax.dynamic_index_in_dim(block, mine, dim, keepdims=False)
    sent = lax.dynamic_index_in_dim(block, 1 - mine, dim, keepdims=False)
    return kept, sent


def along_y(part, rows, along):
    quarter = rows.shape[1] // 4
    joined = jnp.concatenate([part, rows.astype(jnp.bfloat16)], axis=0)
    blocks = by_group([joined[:, j * quarter : (j + 1) * quarter] for j in range(4)], along)
    return [blocks[0]] + [swap(blocks[k], "dp", 2 * k) for k in range(1, 4)]


def first_half_step(quarters, count, ctx):
    total = quarters[0].astype(jnp.float32)
    for block in quarters[1:]:
        total = total + block.astype(jnp.float32)
    rows = total[-count:].astype(jnp.bfloat16)
    part = total[:-count].astype(jnp.bfloat16).reshape(2, 2, 2, 2, -1, total.shape[1])
    kept, sent = pick(part, 3, 2, ctx)
    joined = jnp.concatenate([sent.reshape(-1, total.shape[1]), rows], axis=0)
    return swap(joined, "ctx", 2), kept, rows


def over_columns(part, other, rows, ctx, dp):
    count, quarter = rows.shape
    for dim, mask in ((2, 4), (1, 8), (0, 16), (0, 0)):
        part = add(part, other[:-count].reshape(part.shape))
        rows = rows.astype(jnp.float32) + other[-count:].astype(jnp.float32)
        if mask:
            part, sent = pick(part, dim, mask, ctx)
            rows = rows.astype(jnp.bfloat16)
            other = swap(jnp.concatenate([sent.reshape(-1, quarter), rows], axis=0), "ctx", mask)
    joined = jnp.concatenate([part, rows.astype(jnp.bfloat16)], axis=0)
    total = joined.astype(jnp.float32) + swap(joined, "dp", 1).astype(jnp.float32)
    half = quarter // 2
    weight = jnp.where(bit_of(dp, 1), total[:-count, half:], total[:-count, :half])
    rows = total[-count:]
    spread = [rows] + [swap(rows, "dp", 2 * k) for k in range(1, 4)]
    return weight, jnp.concatenate(by_group(spread, dp // 2), axis=1)


def shards(
    queries, attn_keys, attn_values, residual, out_weight, conv_taps, norm_gain, lengths, cotangent
):
    frames = queries.shape[1]
    width = residual.shape[2]
    ctx = lax.axis_index("ctx")
    dp = lax.axis_index("dp")
    dp_size = lax.axis_size("dp")
    group = (ctx // GROUP_BITS) % GROUPS
    length = lengths[0]

    query_scaled = (queries[0].astype(jnp.float32) * (1.0 / math.sqrt(HD))).astype(jnp.bfloat16)
    pieces = []
    for g in range(GROUPS):
        cols = []
        for h in range(GH):
            first = (g * GH + h) * HD
            cols += [attn_keys[0][:, first : first + HD], attn_values[0][:, first : first + HD]]
        cols.append(query_scaled[:, g * GW : (g + 1) * GW])
        pieces.append(jnp.concatenate(cols, axis=1))
    relative = by_group(pieces, group)
    received = exchange(relative)
    held = jnp.concatenate(by_group(received, group), axis=0)
    own_pairs, query = held[:, : GH * 128], held[:, GH * 128 :]
    rows = own_pairs.shape[0]
    beside = swap(out_weight, "dp", 1)
    core = ctx % 2
    same = (dp % 2) == core
    mine = jnp.where(same, out_weight, beside)
    theirs = jnp.where(same, beside, out_weight)
    own_pairs, mine = lax.optimization_barrier((own_pairs, mine))
    half = rows // 2
    core_own = swap(own_pairs, "ctx", 1)
    from_x = swap(own_pairs, "ctx", MASK_X)
    from_z = swap(own_pairs, "ctx", MASK_Z)
    weight_near = swap(mine, "dp", 2)
    weight_far = swap(mine, "dp", 6)
    order = [0, MASK_X, MASK_Z, MASK_X ^ MASK_Z]
    outside = ctx & ~((GROUPS - 1) * GROUP_BITS)
    starts = jnp.concatenate(
        [
            jnp.stack([((outside ^ k) + g * GROUP_BITS) * frames for g in range(GROUPS)])
            for k in order + [k ^ 1 for k in order]
        ]
    )
    positions = (starts[:, None] + jnp.arange(frames, dtype=jnp.int32)[None, :]).reshape(-1, 1)
    masked = (positions >= length) & (jnp.arange(2 * HD) == HD)[None, :]
    bias = jnp.where(masked, MASK_FILL, 0.0).astype(jnp.bfloat16)
    from_x, from_z, weight_near, weight_far, query, bias = lax.optimization_barrier(
        (from_x, from_z, weight_near, weight_far, query, bias)
    )
    diag_low = swap(from_z[:half], "ctx", MASK_X)
    diag_high = swap(from_x[half:], "ctx", MASK_Z)
    middle = mine.shape[0] // 2
    diag_low, diag_high, weight_near, weight_far = lax.optimization_barrier(
        (diag_low, diag_high, weight_near, weight_far)
    )
    weight_low = swap(weight_near[:middle], "dp", 6)
    weight_high = swap(weight_far[middle:], "dp", 2)
    other_near, other_far = swap(weight_near, "ctx", 1), swap(weight_far, "ctx", 1)
    near = [own_pairs, from_x, from_z, diag_low, diag_high]
    far = [core_own, swap(jnp.concatenate(near[1:], axis=0), "ctx", 1)]

    first_half = attention(query, near, bias, 0)
    first_half, weight_low, weight_high, other_near, other_far, far = lax.optimization_barrier(
        (first_half, weight_low, weight_high, other_near, other_far, far)
    )
    weight_across = jnp.concatenate([weight_low, weight_high], axis=0)
    other_across = swap(weight_across, "ctx", 1)
    att_heads, log_total = attention(query, far, bias, 1, first_half)

    def rows_home(block):
        parts = by_group([block[g * frames : (g + 1) * frames] for g in range(GROUPS)], group)
        back = [parts[0]] + [swap(parts[k], "ctx", k * GROUP_BITS) for k in range(1, GROUPS)]
        return by_group(back, group)

    attended = jnp.concatenate(rows_home(att_heads), axis=1)
    other_across, unused = lax.optimization_barrier((other_across, att_heads))
    mine_rows = by_group([mine, weight_near, weight_across, weight_far], dp // 2)
    other_rows = by_group([theirs, other_near, other_across, other_far], dp // 2)
    ordered = []
    for first, second in zip(mine_rows, other_rows):
        ordered += [jnp.where(core == 1, second, first), jnp.where(core == 1, first, second)]
    weight_all = jnp.concatenate(ordered, axis=0)
    projected = jnp.dot(attended, weight_all, preferred_element_type=jnp.float32)
    residual_mid = (residual[0].astype(jnp.float32) + projected).astype(jnp.bfloat16)
    mid_float = residual_mid.astype(jnp.float32)
    first_frame = ctx * frames
    local_valid = first_frame + jnp.arange(frames, dtype=jnp.int32) < length
    frame_valid = local_valid.astype(jnp.float32)[:, None]
    normed = norm_part(mid_float, norm_gain, frame_valid).astype(jnp.bfloat16)
    side = HALO // 2
    cot = cotangent[0]
    low, high = neighbours(
        jnp.concatenate([normed[:HALO], cot[:side]], axis=0),
        jnp.concatenate([normed[frames - HALO :], cot[frames - side :]], axis=0),
    )
    layer_out, grad_residual, tap_rows = conv_part(
        jnp.clip(length - first_frame, 0, frames).reshape(1),
        normed,
        low,
        high,
        residual_mid,
        cot,
        jnp.concatenate([conv_taps, norm_gain[None]], axis=0),
    )

    grad_att = lax.dot_general(
        grad_residual, weight_all, (((1,), (1,)), ((), ())), preferred_element_type=jnp.float32
    ).astype(jnp.bfloat16)

    parts = by_group([grad_att[:, g * GW : (g + 1) * GW] for g in range(GROUPS)], group)
    moved = [parts[0]] + [swap(parts[k], "ctx", k * GROUP_BITS) for k in range(1, GROUPS)]
    datt = jnp.concatenate(by_group(moved, group), axis=0)

    att_other = swap(attended, "ctx", 1)
    grad_mine, tap_mine, unused = lax.optimization_barrier((grad_residual, tap_rows, grad_att))
    grad_other = swap(grad_mine, "ctx", 1)
    tap_other = swap(tap_mine, "ctx", 1)
    contract = (((0,), (0,)), ((), ()))
    part = lax.dot_general(
        attended, grad_residual, contract, preferred_element_type=jnp.float32
    ) + lax.dot_general(att_other, grad_other, contract, preferred_element_type=jnp.float32)
    part = lax.dynamic_index_in_dim(
        part.reshape(HW // 48, 2, HW // 32, width), ctx % 2, 1, keepdims=False
    ).astype(jnp.bfloat16)
    along = dp // 2
    taps = tap_mine.astype(jnp.float32) + tap_other.astype(jnp.float32)
    quarters = along_y(part.reshape(HW // 2, width), taps, along)

    query_half, far_grad = attention_back(
        query, datt, att_heads, log_total, far, bias, 1, (4 * rows,)
    )
    arrived = swap(far_grad, "ctx", 1)
    query_grad, own, to_x, to_z, far_low, far_high = attention_back(
        query, datt, att_heads, log_total, near, bias, 0,
        (rows, rows, rows, half, half), query_half,
    )
    quarters, unused = lax.optimization_barrier((quarters, own))
    sent, kept, taps = first_half_step(quarters, taps.shape[0], ctx)
    sent, unused = lax.optimization_barrier((sent, arrived))
    grad_weight, tap_sum = over_columns(kept, sent, taps, ctx, dp)
    grad_taps, grad_gain = tap_sum[:KTAPS], tap_sum[KTAPS]

    far_x = swap(add(far_low, arrived[3 * rows : 3 * rows + half]), "ctx", MASK_X)
    far_z = swap(add(far_high, arrived[3 * rows + half :]), "ctx", MASK_Z)
    to_x = to_x.astype(jnp.float32) + arrived[rows : 2 * rows].astype(jnp.float32)
    to_z = to_z.astype(jnp.float32) + arrived[2 * rows : 3 * rows].astype(jnp.float32)
    to_z = jnp.concatenate([to_z[:half] + far_x.astype(jnp.float32), to_z[half:]], axis=0)
    to_x = jnp.concatenate([to_x[:half], to_x[half:] + far_z.astype(jnp.float32)], axis=0)
    pair_sum = (
        own.astype(jnp.float32)
        + arrived[:rows].astype(jnp.float32)
        + swap(to_x.astype(jnp.bfloat16), "ctx", MASK_X).astype(jnp.float32)
        + swap(to_z.astype(jnp.bfloat16), "ctx", MASK_Z).astype(jnp.float32)
    ).astype(jnp.bfloat16)
    home = rows_home(jnp.concatenate([pair_sum, query_grad], axis=1))
    keys_out, values_out, queries_out = [], [], []
    for block in home:
        for h in range(GH):
            keys_out.append(block[:, h * 128 : h * 128 + HD])
            values_out.append(block[:, h * 128 + HD : (h + 1) * 128])
        queries_out.append(block[:, GH * 128 :])
    return (
        layer_out[None],
        jnp.concatenate(queries_out, axis=1)[None],
        jnp.concatenate(keys_out, axis=1)[None],
        jnp.concatenate(values_out, axis=1)[None],
        grad_residual[None],
        grad_weight,
        grad_taps,
        grad_gain,
    )


def solution(mesh):
    placed = (
        P("dp", "ctx", None),
        P("dp", "ctx", None),
        P("dp", "ctx", None),
        P("dp", "ctx", None),
        P("dp", None),
        P(),
        P(),
        P("dp"),
        P("dp", "ctx", None),
    )
    return jax.shard_map(
        shards,
        mesh=mesh,
        in_specs=placed,
        out_specs=(
            P("dp", "ctx", None),
            P("dp", "ctx", None),
            P("dp", "ctx", None),
            P("dp", "ctx", None),
            P("dp", "ctx", None),
            P("ctx", "dp"),
            P(),
            P(),
        ),
        check_vma=False,
    )
```
